256 devices in a mesh: var: 32 (over z, y_lo, core), band: 8 (over x, y_hi).
Axes of the slice: x: 4, y: 4 (y_hi: 2, y_lo: 2; y = y_hi * 2 + y_lo), z: 8, core: 2. Of those that a mesh axis runs over, the one named last changes fastest.
Arguments:
- fields: bfloat16 [64, 256, 1024], P('var', None, 'band'), may hold values from -6 to 6
- stem_in: bfloat16 [64, 16, 512], P('var'), may hold values from -1.5 to 1.5
- stem_out: bfloat16 [64, 512, 512], P('var'), may hold values from -0.25 to 0.25
- level_ids: int32 [64], replicated, may hold values from 0 to 127
- level_table: bfloat16 [128, 512], replicated, may hold values from -6 to 6
- latent_query: bfloat16 [4, 512], replicated, may hold values from -100 to 100
- kv_weight: bfloat16 [512, 1024], replicated, may hold values from -0.25 to 0.25
- out_weight: bfloat16 [512, 512], replicated, may hold values from -0.25 to 0.25
- region_ids: int32 [32, 128], replicated, may hold values from 0 to 255, as said below
Outputs:
- latents: bfloat16 [64, 256, 4, 512], P('var', 'band')
- region_means: float32 [256, 4, 512], P(('var', 'band'))
The draws below stay inside these ranges and needn't reach their ends.
Inputs may be any that keep to these rules, and one draw needn't show every extreme that they name: `region_ids`: every region 0 to 255 holds at least one coarse cell; within each aligned block of 1 coarse rows and 16 coarse columns, every region that occurs occurs exactly 2 times.
All inputs are finite; a program needn't handle non-finite values.
Results may differ from the reference program's by a relative error of at most 0.0065.
Values may be sent and summed in bfloat16 or wider, within the bound.
A program may use at most 64 MiB of HBM per device.

```python
import jax
import jax.numpy as jnp
from jax import lax

D = 512
HEADS = 16
HEAD = 32
LATENT = 4
PATCH = 4
LATP_DEV = 2
LONP_DEV = 32
LEVTAB = 128
CAP = 2
VARS = 64
LATP = 64
LONP = 256
LAT = 256
LON = 1024
R = 256


def draw_latent_query(key, part):
    key = jax.random.fold_in(key, 11)
    values = jnp.clip(jax.random.normal(key, (LATENT, D), jnp.float32), -4.0, 4.0)
    return values.astype(jnp.bfloat16)


def draw_region_ids(key, part):
    key = jax.random.fold_in(key, 23)
    first, second = jax.random.split(key)
    crow = LATP_DEV // 2
    ccol = LONP_DEV // 2
    nrow = LATP // LATP_DEV
    ncol = LONP // LONP_DEV
    cells = crow * ccol
    distinct = cells // CAP
    owners = jax.random.permutation(first, R).astype(jnp.int32)
    device_keys = jax.random.split(second, nrow * ncol)

    def one_device(device_key, own):
        pick_key, mix_key = jax.random.split(device_key)
        offsets = jax.random.permutation(pick_key, R - 1)[:distinct - 1].astype(jnp.int32) + 1
        chosen = jnp.concatenate([own[None], (own + offsets) % R]).astype(jnp.int32)
        labels = jnp.repeat(chosen, CAP)
        return jax.random.permutation(mix_key, labels).astype(jnp.int32)
    labels = jax.vmap(one_device)(device_keys, owners[:nrow * ncol])
    grid = labels.reshape(nrow, ncol, crow, ccol).transpose(0, 2, 1, 3)
    return grid.reshape(LATP // 2, LONP // 2).astype(jnp.int32)


def plant(result, rng, low, top_value):
    spot = [jax.random.randint(jax.random.fold_in(rng, axis), (), 0, length) for axis, length in enumerate(result.shape)]
    longest = result.shape.index(max(result.shape))
    next_to = spot[:longest] + [(spot[longest] + 1) % result.shape[longest]] + spot[longest + 1:]
    return result.at[tuple(spot)].set(low).at[tuple(next_to)].set(top_value)


def steps_of(rng, shape, pieces, least, top_value):
    def one(dim, parts):
        heights = jax.random.uniform(jax.random.fold_in(jax.random.fold_in(rng, 6), dim), (parts,), jnp.float32, least / len(pieces), top_value / len(pieces))
        return jnp.repeat(jnp.exp(heights), shape[dim] // parts).reshape((-1,) + (1,) * (len(shape) - dim - 1))

    level = one(*pieces[0])
    for cut in pieces[1:]:
        level = level * one(*cut)
    return level


def centred(own_key, dims, deviation, limit, shards=(), kind=jnp.bfloat16):
    values = deviation * jax.random.normal(own_key, dims, jnp.float32)
    if shards:
        values = values * steps_of(own_key, dims, shards, -0.22, 0.18)
    return jnp.clip(values, -limit, limit).astype(kind)


def setup_inputs(seed: int = 0) -> dict:
    key_of = jax.random.split(jax.random.key(seed), 10)
    return {
        "fields": centred(key_of[0], (VARS, LAT, LON), 1.0, 6.0, ((0, 32), (2, 8))),
        "stem_in": centred(key_of[1], (VARS, PATCH * PATCH, D), (PATCH * PATCH) ** -0.5, 1.5, ((0, 32),)),
        "stem_out": centred(key_of[2], (VARS, D, D), D ** -0.5, 0.25, ((0, 32),)),
        "level_ids": plant(jax.random.randint(key_of[3], (VARS,), 0, LEVTAB), jax.random.fold_in(key_of[3], 1), 0, LEVTAB - 1).astype(jnp.int32),
        "level_table": centred(key_of[4], (LEVTAB, D), 1.0, 6.0),
        "latent_query": draw_latent_query(jax.random.fold_in(key_of[9], 71), 0),
        "kv_weight": centred(key_of[6], (D, 2 * D), D ** -0.5, 0.25),
        "out_weight": centred(key_of[7], (D, D), D ** -0.5, 0.25),
        "region_ids": draw_region_ids(jax.random.fold_in(key_of[9], 71), 0),
    }


def reference(fields, stem_in, stem_out, level_ids, level_table, latent_query, kv_weight, out_weight, region_ids):
    nvar = fields.shape[0]
    rows = fields.shape[1] // PATCH
    cols = fields.shape[2] // PATCH
    onehot = (level_ids[:, None] == jnp.arange(LEVTAB, dtype=jnp.int32)[None, :]).astype(jnp.bfloat16)
    level_embed = jnp.dot(onehot, level_table, preferred_element_type=jnp.float32)
    stem_in32 = stem_in.astype(jnp.float32)
    stem_out32 = stem_out.astype(jnp.float32)
    kv32 = kv_weight.astype(jnp.float32)
    query32 = latent_query.astype(jnp.float32).reshape(LATENT, HEADS, HEAD)
    scale = 1.0 / HEAD ** 0.5

    def one_row(index):
        strip = lax.dynamic_slice_in_dim(fields, index * PATCH, PATCH, 1)
        pixels = strip.reshape(nvar, PATCH, cols, PATCH).transpose(0, 2, 1, 3).reshape(nvar, cols, PATCH * PATCH)
        stem = jax.nn.gelu(jnp.einsum('vcp,vpd->vcd', pixels.astype(jnp.float32), stem_in32)).astype(jnp.bfloat16)
        tokens = jnp.einsum('vcd,vde->vce', stem.astype(jnp.float32), stem_out32).astype(jnp.bfloat16)
        keyed = tokens.astype(jnp.float32) + level_embed[:, None, :]
        centre = lax.optimization_barrier(jnp.mean(keyed, axis=-1, keepdims=True))
        spread = lax.optimization_barrier(jnp.mean((keyed - centre) ** 2, axis=-1, keepdims=True))
        normed = ((keyed - centre) * lax.rsqrt(spread + 1e-05)).astype(jnp.bfloat16)
        kv = jnp.einsum('vcd,de->vce', normed.astype(jnp.float32), kv32).astype(jnp.bfloat16)
        keys = kv[..., :D].astype(jnp.float32).reshape(nvar, cols, HEADS, HEAD)
        values = kv[..., D:].astype(jnp.float32).reshape(nvar, cols, HEADS, HEAD)
        scores = jnp.einsum('lhe,vche->chlv', query32, keys) * scale
        weights = jax.nn.softmax(scores, axis=-1).astype(jnp.bfloat16)
        mixed = jnp.einsum('chlv,vche->clhe', weights.astype(jnp.float32), values).astype(jnp.bfloat16)
        projected = jnp.dot(mixed.reshape(cols * LATENT, D), out_weight, preferred_element_type=jnp.float32)
        out = latent_query.astype(jnp.float32)[None] + projected.reshape(cols, LATENT, D)
        return out.astype(jnp.bfloat16)
    latents = lax.map(one_row, jnp.arange(rows, dtype=jnp.int32))
    coarse = latents.astype(jnp.float32).reshape(rows // 2, 2, cols // 2, 2, LATENT, D).mean(axis=(1, 3)).astype(jnp.bfloat16)
    flat = coarse.reshape(-1, LATENT * D)
    cells = region_ids.reshape(-1)
    select = jnp.arange(R, dtype=jnp.int32)[:, None] == cells[None, :]
    sums = jnp.dot(select.astype(jnp.bfloat16), flat, preferred_element_type=jnp.float32)
    counts = lax.optimization_barrier(jnp.sum(select.astype(jnp.float32), axis=1))
    region_means = (sums / counts[:, None]).reshape(R, LATENT, D)
    return (latents, region_means)
```

```python
import jax
import jax.numpy as jnp
from jax import lax
from jax.experimental import pallas as pl
from jax.experimental.pallas import tpu as pltpu
from jax.sharding import PartitionSpec as P

MESH = pl.DeviceIdType.MESH
BF16 = jnp.bfloat16
F32 = jnp.float32
I32 = jnp.int32

HEADS = 16
HEAD = 32
WIDTH = 512
LATENT = 4
FLAT = LATENT * WIDTH
NZ = 8
GROUP = 4
NVAR = 32
NBAND = 8
CHUNK = 64
HALF = 32
LOG2E = 1.4426950408889634
PIECE = 128


def iota(shape, axis):
    return lax.broadcasted_iota(I32, shape, axis)


def dot(a, b):
    return jnp.dot(a, b, preferred_element_type=F32)


def dot_nt(a, b):
    return lax.dot_general(a, b, (((1,), (1,)), ((), ())), preferred_element_type=F32)


def mod(a, n):
    return lax.rem(a, jnp.int32(n))


def div(a, n):
    return lax.div(a, jnp.int32(n))


def kernel(
    fields, stem_in, stem_out, ids_hbm, table_hbm, query_hbm, kvw_hbm, outw_hbm, regions_hbm,
    lat, means,
    field_v, ids, table, query, kvw, outw, regions,
    pbuf, pown, sbuf, wbuf, fscr, lhs, tile, normed, emb, qk, ex,
    part, ms, rpart, rms, chosen, pairs, table_f, table_b, rows,
    lsem, ps, pr, ss, sr, ws, wr, xs, fs, os, orr, mss, msr, cs, cr, ts, tr,
):
    vi = lax.axis_index("var")
    bi = lax.axis_index("band")
    z = div(vi, GROUP)
    g = mod(vi, GROUP)
    ylo = div(g, 2)
    core = mod(g, 2)
    x = div(bi, 2)
    yhi = mod(bi, 2)
    y = yhi * 2 + ylo
    odd_x = mod(x, 2)
    base = z * GROUP
    g_core = ylo * 2 + 1 - core
    g_y = (1 - ylo) * 2 + core
    g_diag = (1 - ylo) * 2 + 1 - core
    core_dev = (base + g_core, bi)
    band_next = x * 2 + div(mod(y + 1, 4), 2)
    band_prev = x * 2 + div(mod(y + 3, 4), 2)
    band_far = x * 2 + 1 - yhi
    right = (vi, mod(x + 1, 4) * 2 + yhi)
    left = (vi, mod(x + 3, 4) * 2 + yhi)
    member = g * 2 + yhi
    place = z * 4 + x

    def member_dev(j):
        other = mod(member + j, 8)
        return (base + div(other, 2), x * 2 + mod(other, 2))

    def place_dev(j):
        other = mod(place + j, NVAR)
        return (div(other, 4) * GROUP + g, mod(other, 4) * 2 + yhi)

    barrier = pltpu.get_barrier_semaphore()

    def greet_member(j, carry):
        pl.semaphore_signal(barrier, inc=1, device_id=member_dev(j), device_id_type=MESH)
        return carry

    def greet_place(j, carry):
        pl.semaphore_signal(barrier, inc=1, device_id=place_dev(j), device_id_type=MESH)
        return carry

    lax.fori_loop(1, NVAR, greet_place, 0)
    lax.fori_loop(1, 8, greet_member, 0)

    local_copies = [
        pltpu.make_async_copy(src, dst, lsem.at[k])
        for k, (src, dst) in enumerate((
            (fields, field_v), (stem_out, wbuf.at[0]), (stem_in, sbuf.at[0]), (ids_hbm, ids),
            (table_hbm, table), (query_hbm, query), (kvw_hbm, kvw), (regions_hbm, regions),
            (outw_hbm, outw),
        ))
    ]
    for copy in local_copies:
        copy.start()

    local_copies[0].wait()
    ff = field_v[...].astype(F32).reshape(2, NZ, GROUP, 8, 128)
    for k in range(GROUP):
        pown[k] = ff[:, :, k].reshape(2 * NZ * 8, 128).astype(BF16)
    pbuf[0] = pown[g]

    pl.semaphore_wait(barrier, NVAR - 1 + 7)

    def piece_copy(src, s, u, j, send, target):
        start = pl.multiple_of(j * PIECE, PIECE)
        return pltpu.make_async_remote_copy(
            src_ref=src.at[u, pl.ds(start, PIECE), :], dst_ref=wbuf.at[s, u, pl.ds(start, PIECE), :],
            send_sem=send, recv_sem=wr.at[s, u, j], device_id=target, device_id_type=MESH,
        )

    def whole_copy(u, send):
        return pltpu.make_async_remote_copy(
            src_ref=stem_out.at[u], dst_ref=wbuf.at[1, u], send_sem=send,
            recv_sem=wr.at[1, u, 0], device_id=core_dev, device_id_type=MESH,
        )

    def pixel_copy(k, source, target):
        return pltpu.make_async_remote_copy(
            src_ref=pown.at[source], dst_ref=pbuf.at[k + 1], send_sem=ps.at[k],
            recv_sem=pr.at[k], device_id=target, device_id_type=MESH,
        )

    def stem_copy(k, target):
        return pltpu.make_async_remote_copy(
            src_ref=stem_in, dst_ref=sbuf.at[k + 1], send_sem=ss.at[k],
            recv_sem=sr.at[k], device_id=target, device_id_type=MESH,
        )

    next_dev = (base + g_y, band_next)
    prev_dev = (base + g_y, band_prev)
    sends = [
        pixel_copy(0, g_core, core_dev),
        stem_copy(0, core_dev),
        whole_copy(0, ws.at[4]),
        piece_copy(stem_out, 2, odd_x, 0, ws.at[0], next_dev),
        piece_copy(stem_out, 2, odd_x, 2, ws.at[2], prev_dev),
        whole_copy(1, ws.at[5]),
        pixel_copy(1, g_y, (base + g_y, bi)),
        stem_copy(1, (base + g_y, band_far)),
        piece_copy(stem_out, 2, odd_x, 1, ws.at[1], next_dev),
        piece_copy(stem_out, 2, odd_x, 3, ws.at[3], prev_dev),
        pixel_copy(2, g_diag, (base + g_diag, bi)),
        stem_copy(2, (base + g_diag, band_far)),
    ]
    for copy in sends:
        copy.start()

    def forward_x(j, target):
        return piece_copy(wbuf.at[2], 2, odd_x, j, xs.at[j], target)

    def forward_core(u, j):
        return pltpu.make_async_remote_copy(
            src_ref=wbuf.at[2, u, pl.ds(j * PIECE, PIECE), :],
            dst_ref=wbuf.at[3, u, pl.ds(j * PIECE, PIECE), :],
            send_sem=fs.at[u, j], recv_sem=wr.at[3, u, j], device_id=core_dev, device_id_type=MESH,
        )

    def arrived(s, u, j):
        piece_copy(stem_out, s, u, j, ws.at[0], core_dev).wait_recv()

    def from_y(j_right, j_left):
        arrived(2, odd_x, j_right)
        forward_x(j_right, right).start()
        forward_core(odd_x, j_right).start()
        arrived(2, odd_x, j_left)
        forward_x(j_left, left).start()
        forward_core(odd_x, j_left).start()

    def from_x(first, second):
        for j in (first, second):
            arrived(2, 1 - odd_x, j)
            forward_core(1 - odd_x, j).start()

    tile[...] = (
        (div(iota((512, 128), 0), 128) == div(iota((512, 128), 1), 4))
        & (mod(iota((512, 128), 0), 4) == mod(iota((512, 128), 1), 4))
    ).astype(F32).astype(BF16)
    for l in range(LATENT):
        lane = iota((128, 1024), 1)
        want = div(mod(lane, WIDTH), HEAD) + l * HEADS + div(lane, WIDTH) * 64
        ex[l] = (iota((128, 1024), 0) == want).astype(F32).astype(BF16)
    for copy in local_copies[3:5]:
        copy.wait()
    onehot = (iota((128, 64), 0) == ids[...]).astype(F32)
    emb[...] = dot(onehot.T.astype(BF16), table[...])
    for copy in local_copies[5:8]:
        copy.wait()
    qf = query[...].astype(F32)
    heads = iota((HEADS, WIDTH), 0) == div(iota((HEADS, WIDTH), 1), HEAD)
    qmat = jnp.concatenate(
        [jnp.where(heads, jnp.broadcast_to(qf[l:l + 1], (HEADS, WIDTH)), 0.0) for l in range(LATENT)],
        axis=0,
    ).astype(BF16)
    folded = dot_nt(qmat, kvw[:, :WIDTH]) * (LOG2E / HEAD**0.5)
    high = folded.astype(BF16).astype(F32)
    qk[...] = jnp.concatenate([high, folded - high], axis=0).T.astype(BF16)

    ones = jnp.ones((128, 128), F32)
    same_tile = div(iota((128, 128), 0), 16) == div(iota((128, 128), 1), 16)
    slot_row = iota((128, 128), 0)
    tile_lane = div(iota((128, 128), 1), 16)
    dest = iota((NVAR, 128), 0)
    dest_region = (div(dest, 4) * GROUP + g) * NBAND + mod(dest, 4) * 2 + yhi
    picked = jnp.zeros((NVAR, 128), F32)

    def slots(row):
        across = row.astype(F32) * ones
        below = jnp.where((across.T < across) & same_tile, 0.5, 0.0)
        return jnp.sum(below, axis=0, keepdims=True).astype(I32)

    for k in range(GROUP):
        row = regions[pl.ds(base + k, 1), :]
        hit = (slots(row) == mod(slot_row, 8)) & (div(slot_row, 32) == k) & (
            tile_lane == x * 2 + mod(div(slot_row, 16), 2)
        )
        in_region = (row == dest_region).astype(F32).astype(BF16)
        picked = picked + dot_nt(in_region, jnp.where(hit, 0.5, 0.0).astype(BF16))
    upper = mod(div(iota((NVAR, 128), 1), 8), 2) == 1
    chosen[...] = jnp.concatenate(
        [jnp.where(upper, 0.0, picked), jnp.where(upper, picked, 0.0)], axis=0
    ).astype(BF16)
    own_row = regions[pl.ds(vi, 1), :]
    own_hit = (slots(own_row) == iota((8, 128), 0)) & (div(iota((8, 128), 1), 16) == bi)
    cell = div(mod(iota((128, CHUNK), 1), HALF), 2)
    average = jnp.where(mod(iota((128, CHUNK), 0), 16) == cell, 0.25, 0.0).astype(BF16)
    pair_mean = dot(own_hit.astype(F32).astype(BF16), average).astype(BF16)
    region = vi * NBAND + bi
    count = jnp.sum((regions[...] == region).astype(F32))

    local_copies[1].wait()
    local_copies[2].wait()
    patch_mask = div(iota((HALF, 128), 1), 4) == iota((HALF, 128), 0)

    def one_variable(t, carry):
        late = div(t, 4)
        s = (1 - late) * div(t, 2) + late * (2 + mod(t, 2))
        second = div(t, 6)
        u = (1 - late) * mod(t, 2) + late * (odd_x + second - 2 * odd_x * second)

        @pl.when(t == 2)
        def _():
            pixel_copy(0, 0, core_dev).wait_recv()
            stem_copy(0, core_dev).wait_recv()
            whole_copy(0, ws.at[4]).wait_recv()

        @pl.when(t == 3)
        def _():
            from_y(0, 2)
            whole_copy(1, ws.at[5]).wait_recv()

        @pl.when(t == 4)
        def _():
            from_y(3, 1)
            pixel_copy(1, 0, core_dev).wait_recv()
            stem_copy(1, core_dev).wait_recv()

        @pl.when(t == 5)
        def _():
            from_x(0, 2)
            pixel_copy(2, 0, core_dev).wait_recv()
            stem_copy(2, core_dev).wait_recv()

        @pl.when(t == 6)
        def _():
            from_x(3, 1)

        @pl.when((t == 5) | (t == 7))
        def _():
            for j in range(4):
                arrived(3, u, j)

        fscr[...] = pbuf[s, pl.ds(pl.multiple_of(u * CHUNK, CHUNK), CHUNK), :].astype(F32)
        for a in range(16):
            for i in range(4):
                row = jnp.broadcast_to(fscr[pl.ds(a * 4 + i, 1), :], (HALF, 128))
                lhs[pl.ds(a * HALF, HALF), pl.ds(i * 128, 128)] = jnp.where(
                    patch_mask, row, 0.0
                ).astype(BF16)
        pixels = dot(lhs[...], tile[...]).astype(BF16)[:, :16]
        x = dot(pixels, sbuf[s, u])
        stem = (0.5 * x * (1.0 + jnp.tanh(0.7978845608028654 * (x + 0.044715 * (x * x * x))))).astype(BF16)
        tokens = dot(stem, wbuf[s, u]).astype(BF16).astype(F32)
        src_g = mod(s, 2)
        src_core = core + src_g - 2 * core * src_g
        up = div(s, 2)
        src_y = ylo + up - 2 * ylo * up
        var = (base + src_y * 2 + src_core) * 2 + u
        keyed = tokens + emb[pl.ds(var, 1), :]
        centre = jnp.mean(keyed, axis=-1, keepdims=True)
        away = keyed - centre
        spread = jnp.mean(away * away, axis=-1, keepdims=True)
        normed[t] = (away * lax.rsqrt(spread + 1e-05)).astype(BF16)
        return carry

    lax.fori_loop(0, 8, one_variable, 0)

    low_lanes = iota((CHUNK, 128), 1) < 64

    def ring_copies(dr, d, half):
        off = mod(d + dr * (8 - 2 * d), 8)
        target = (mod(z + 1 + 6 * dr, NZ) * GROUP + g, bi)
        start = pl.multiple_of(half * HALF, HALF)
        return (
            pltpu.make_async_remote_copy(
                src_ref=ms.at[off, pl.ds(start, HALF), :], dst_ref=rms.at[dr, d - 1, half],
                send_sem=mss.at[dr, d - 1, half], recv_sem=msr.at[dr, d - 1, half],
                device_id=target, device_id_type=MESH,
            ),
            pltpu.make_async_remote_copy(
                src_ref=part.at[off, pl.ds(start, HALF), :], dst_ref=rpart.at[dr, d - 1, half],
                send_sem=os.at[dr, d - 1, half], recv_sem=orr.at[dr, d - 1, half],
                device_id=target, device_id_type=MESH,
            ),
        )

    def ring_send(dr, d, half):
        for copy in ring_copies(dr, d, half):
            copy.start()

    def local(off):
        start = pl.multiple_of(mod(z + off, NZ) * CHUNK, CHUNK)
        nb = normed[:, pl.ds(start, CHUNK), :].reshape(8 * CHUNK, WIDTH)
        scores = dot(nb, qk[...])
        scores = (scores + pltpu.roll(scores, 64, 1)).reshape(8, CHUNK, 128)
        top = jnp.ceil(jnp.max(scores, axis=0))
        p = jnp.exp2(scores - top[None])
        ms[off] = jnp.where(low_lanes, top, jnp.sum(p, axis=0))
        pb = p.astype(BF16).reshape(8 * CHUNK, 128)
        values = dot(nb, kvw[:, WIDTH:])
        for l in range(LATENT):
            wide = dot(pb, ex[l, :, :WIDTH])
            part[off, :, l * WIDTH:(l + 1) * WIDTH] = jnp.sum(
                (wide * values).reshape(8, CHUNK, WIDTH), axis=0
            ).astype(BF16)

    def offset(dr, d):
        return mod(d + dr * (8 - 2 * d), 8)

    def merge(d, half):
        parts = []
        for dr, h in ((0, half), (1, 1 - half)):
            parts.append((dr, h, offset(dr, d), pl.ds(pl.multiple_of(h * HALF, HALF), HALF)))
        mine = jnp.concatenate([ms[off, at, :] for _, _, off, at in parts], axis=0)
        other = jnp.concatenate([rms[dr, d, h] for dr, h, _, _ in parts], axis=0)
        mine_r = pltpu.roll(mine, 64, 1)
        other_r = pltpu.roll(other, 64, 1)
        m1 = jnp.where(low_lanes, mine, mine_r)
        s1 = jnp.where(low_lanes, mine_r, mine)
        m2 = jnp.where(low_lanes, other, other_r)
        s2 = jnp.where(low_lanes, other_r, other)
        m = jnp.maximum(m1, m2)
        a1 = jnp.exp2(m1 - m)
        a2 = jnp.exp2(m2 - m)
        new = jnp.where(low_lanes, m, a1 * s1 + a2 * s2)
        ab = jnp.where(low_lanes, a2, a1).astype(BF16)
        for k, (_, _, off, at) in enumerate(parts):
            ms[off, at, :] = new[k * HALF:(k + 1) * HALF]
        for l in range(LATENT):
            cols = slice(l * WIDTH, (l + 1) * WIDTH)
            factor = dot(ab, ex[l])
            for k, (dr, h, off, at) in enumerate(parts):
                lines = slice(k * HALF, (k + 1) * HALF)
                part[off, at, cols] = (
                    factor[lines, :WIDTH] * rpart[dr, d, h, :, cols].astype(F32)
                    + factor[lines, WIDTH:] * part[off, at, cols].astype(F32)
                ).astype(BF16)

    def merge_step(d):
        def one(i, carry):
            half = 1 - i

            @pl.when((d < 3) | (i > 0))
            def _():
                for dr, h in ((0, half), (1, i)):
                    for copy in ring_copies(dr, d + 1, h):
                        copy.wait_recv()
                merge(d, half)

            @pl.when(d > 0)
            def _():
                ring_send(0, d, half)
                ring_send(1, d, i)

            return carry

        lax.fori_loop(0, 2, one, 0)

    def one_chunk(k, carry):
        odd = mod(k, 2)
        local(4 - div(k + 1, 2) * odd + div(k, 2) * (1 - odd))

        @pl.when(k == 0)
        def _():
            ring_send(0, 4, 0)
            ring_send(1, 4, 1)

        @pl.when((odd == 0) & (k > 0))
        def _():
            merge_step(4 - div(k, 2))

        return carry

    lax.fori_loop(0, 7, one_chunk, 0)
    local(0)
    merge_step(0)

    total = ms[0]
    inverse = 1.0 / jnp.where(low_lanes, pltpu.roll(total, 64, 1), total)
    inv_high = inverse.astype(BF16).astype(F32)
    inv = jnp.where(low_lanes, inv_high, inverse - inv_high).astype(BF16)
    mixed = []
    for l in range(LATENT):
        factor = dot(inv, ex[l])
        mixed.append(
            (part[0, :, l * WIDTH:(l + 1) * WIDTH].astype(F32)
             * (factor[:, :WIDTH] + factor[:, WIDTH:])).astype(BF16)
        )
    local_copies[8].wait()
    projected = dot(jnp.concatenate(mixed, axis=0), outw[...])
    sums = []
    for l in range(LATENT):
        cols = slice(l * WIDTH, (l + 1) * WIDTH)
        out = (projected[l * CHUNK:(l + 1) * CHUNK] + qf[l:l + 1]).astype(BF16)
        lat[:, cols] = out
        sums.append(dot(pair_mean, out))
    pairs[member] = jnp.concatenate(
        [jnp.concatenate(sums[:2], axis=1), jnp.concatenate(sums[2:], axis=1)], axis=0
    ).astype(BF16)

    def pair_copy(j, slot):
        return pltpu.make_async_remote_copy(
            src_ref=pairs.at[slot], dst_ref=pairs.at[slot], send_sem=cs.at[j], recv_sem=cr.at[j],
            device_id=member_dev(j), device_id_type=MESH,
        )

    def pair_send(j, carry):
        pair_copy(j, member).start()
        return carry

    def pair_wait(j, carry):
        pair_copy(j, mod(member + 8 - j, 8)).wait_recv()
        return carry

    lax.fori_loop(1, 8, pair_send, 0)
    lax.fori_loop(1, 8, pair_wait, 0)
    by_dest = dot(chosen[...], pairs[...].reshape(128, 2 * WIDTH))
    for k in range(16):
        table_f[:, k, :] = by_dest[(k // 8) * NVAR:(k // 8 + 1) * NVAR, (k % 8) * 128:(k % 8 + 1) * 128]
    table_b[...] = table_f[...].astype(BF16)

    def row_copy(j):
        return pltpu.make_async_remote_copy(
            src_ref=table_b.at[mod(place + j, NVAR)], dst_ref=rows.at[j], send_sem=ts.at[j],
            recv_sem=tr.at[j], device_id=place_dev(j), device_id_type=MESH,
        )

    def row_send(j, carry):
        row_copy(j).start()
        return carry

    def row_wait(j, carry):
        row_copy(j).wait_recv()
        return carry

    lax.fori_loop(1, NVAR, row_send, 0)
    rows[0] = table_b[place]
    lax.fori_loop(1, NVAR, row_wait, 0)
    total = jnp.sum(rows[...].astype(F32), axis=0) / count
    for l in range(LATENT):
        for k in range(4):
            means[0, l:l + 1, k * 128:(k + 1) * 128] = total[l * 4 + k:l * 4 + k + 1, :]

    for copy in sends:
        copy.wait_send()
    for j in range(4):
        forward_x(j, right).wait_send()
        forward_core(0, j).wait_send()
        forward_core(1, j).wait_send()

    def ring_over(i, carry):
        dr = mod(i, 2)
        half = mod(div(i, 2), 2)
        d = 1 + div(i, 4)

        @pl.when((d < 4) | (half == dr))
        def _():
            for copy in ring_copies(dr, d, half):
                copy.wait_send()

        return carry

    def pair_over(j, carry):
        pair_copy(j, member).wait_send()
        return carry

    def row_over(j, carry):
        row_copy(j).wait_send()
        return carry

    lax.fori_loop(0, 16, ring_over, 0)
    lax.fori_loop(1, 8, pair_over, 0)
    lax.fori_loop(1, NVAR, row_over, 0)


def shards(fields, stem_in, stem_out, level_ids, level_table, latent_query, kv_weight, out_weight, region_ids):
    vmem = pl.BlockSpec(memory_space=pltpu.VMEM)
    dma = pltpu.SemaphoreType.DMA
    lat, means = pl.pallas_call(
        kernel,
        out_shape=(
            jax.ShapeDtypeStruct((CHUNK, FLAT), BF16),
            jax.ShapeDtypeStruct((1, LATENT, WIDTH), F32),
        ),
        in_specs=[pl.BlockSpec(memory_space=pl.ANY)] * 9,
        out_specs=(vmem, vmem),
        scratch_shapes=[
            pltpu.VMEM((2, 256, 128), BF16),
            pltpu.VMEM((1, 64), I32),
            pltpu.VMEM((128, WIDTH), BF16),
            pltpu.VMEM((LATENT, WIDTH), BF16),
            pltpu.VMEM((WIDTH, 2 * WIDTH), BF16),
            pltpu.VMEM((WIDTH, WIDTH), BF16),
            pltpu.VMEM((32, 128), I32),
            pltpu.VMEM((GROUP, 128, 128), BF16),
            pltpu.VMEM((GROUP, 128, 128), BF16),
            pltpu.VMEM((GROUP, 2, 16, WIDTH), BF16),
            pltpu.VMEM((GROUP, 2, WIDTH, WIDTH), BF16),
            pltpu.VMEM((CHUNK, 128), F32),
            pltpu.VMEM((512, 512), BF16),
            pltpu.VMEM((512, 128), BF16),
            pltpu.VMEM((8, 512, WIDTH), BF16),
            pltpu.VMEM((64, WIDTH), F32),
            pltpu.VMEM((WIDTH, 128), BF16),
            pltpu.VMEM((LATENT, 128, 2 * WIDTH), BF16),
            pltpu.VMEM((NZ, CHUNK, FLAT), BF16),
            pltpu.VMEM((NZ, CHUNK, 128), F32),
            pltpu.VMEM((2, 4, 2, HALF, FLAT), BF16),
            pltpu.VMEM((2, 4, 2, HALF, 128), F32),
            pltpu.VMEM((2 * NVAR, 128), BF16),
            pltpu.VMEM((8, 16, 2 * WIDTH), BF16),
            pltpu.VMEM((NVAR, 16, 128), F32),
            pltpu.VMEM((NVAR, 16, 128), BF16),
            pltpu.VMEM((NVAR, 16, 128), BF16),
            dma((9,)),
            dma((3,)), dma((3,)),
            dma((3,)), dma((3,)),
            dma((6,)), dma((GROUP, 2, 4)), dma((4,)), dma((2, 4)),
            dma((2, 4, 2)), dma((2, 4, 2)),
            dma((2, 4, 2)), dma((2, 4, 2)),
            dma((8,)), dma((8,)),
            dma((NVAR,)), dma((NVAR,)),
        ],
        compiler_params=pltpu.CompilerParams(
            collective_id=0, has_side_effects=True, vmem_limit_bytes=60 * 1024 * 1024
        ),
        name="window",
    )(
        fields, stem_in, stem_out, level_ids.reshape(1, -1), level_table, latent_query,
        kv_weight, out_weight, region_ids,
    )
    return lat.reshape(2, 32, LATENT, WIDTH), means


def solution(mesh):
    in_specs = (
        P("var", None, "band"),
        P("var", None, None),
        P("var", None, None),
        P(),
        P(),
        P(),
        P(),
        P(),
        P(),
    )
    out_specs = (P("var", "band", None, None), P(("var", "band"), None, None))
    return jax.shard_map(shards, mesh=mesh, in_specs=in_specs, out_specs=out_specs, check_vma=False)
```

```python
import jax
import jax.numpy as jnp
from jax import lax
from jax.experimental import pallas as pl
from jax.experimental.pallas import tpu as pltpu
from jax.sharding import PartitionSpec as P

MESH = pl.DeviceIdType.MESH
BF16 = jnp.bfloat16
F32 = jnp.float32
I32 = jnp.int32

HEADS = 16
HEAD = 32
WIDTH = 512
LATENT = 4
FLAT = LATENT * WIDTH
NZ = 8
GROUP = 4
NVAR = 32
NBAND = 8
CHUNK = 64
HALF = 32
LOG2E = 1.4426950408889634
PIECES = ((0, 128), (128, 128), (256, 64), (320, 64), (384, 64), (448, 64))


def iota(shape, axis):
    return lax.broadcasted_iota(I32, shape, axis)


def dot(a, b):
    return jnp.dot(a, b, preferred_element_type=F32)


def dot_nt(a, b):
    return lax.dot_general(a, b, (((1,), (1,)), ((), ())), preferred_element_type=F32)


def mod(a, n):
    return lax.rem(a, jnp.int32(n))


def div(a, n):
    return lax.div(a, jnp.int32(n))


def kernel(
    fields, stem_in, stem_out, ids_hbm, table_hbm, query_hbm, kvw_hbm, outw_hbm, regions_hbm,
    lat, means,
    field_v, ids, table, query, kvw, outw, regions,
    pbuf, pown, sbuf, wbuf, fscr, lhs, tile, normed, emb, qk, ex,
    part, ms, rpart, rms, chosen, pairs, table_f, table_b, rows,
    lsem, ps, pr, ss, sr, ws, wr, xs, fs, os, orr, mss, msr, cs, cr, ts, tr,
):
    vi = lax.axis_index("var")
    bi = lax.axis_index("band")
    z = div(vi, GROUP)
    g = mod(vi, GROUP)
    ylo = div(g, 2)
    core = mod(g, 2)
    x = div(bi, 2)
    yhi = mod(bi, 2)
    y = yhi * 2 + ylo
    odd_x = mod(x, 2)
    base = z * GROUP
    g_core = ylo * 2 + 1 - core
    g_y = (1 - ylo) * 2 + core
    g_diag = (1 - ylo) * 2 + 1 - core
    core_dev = (base + g_core, bi)
    band_next = x * 2 + div(mod(y + 1, 4), 2)
    band_prev = x * 2 + div(mod(y + 3, 4), 2)
    band_far = x * 2 + 1 - yhi
    right = (vi, mod(x + 1, 4) * 2 + yhi)
    left = (vi, mod(x + 3, 4) * 2 + yhi)
    member = g * 2 + yhi

    def flip(bit, by):
        return mod(bit + by, 2)

    def member_dev(j):
        other = flip(ylo, j // 4) * 2 + flip(core, (j // 2) % 2)
        return (base + other, x * 2 + flip(yhi, j % 2))

    def place_off(i):
        a, b = div(i, 4), mod(i, 4)
        da = 4 - div(a + 1, 2) * mod(a, 2) + div(a, 2) * (1 - mod(a, 2))
        db = 2 - div(b + 1, 2) * mod(b, 2) + div(b, 2) * (1 - mod(b, 2))
        return mod(z + da, NZ), mod(x + db, 4)

    barrier = pltpu.get_barrier_semaphore()
    near = [member_dev(j) for j in range(1, 8)]
    near += [(vi, mod(x + j, 4) * 2 + yhi) for j in range(1, 4)]
    near += [(mod(z + j, NZ) * GROUP + g, bi) for j in (1, NZ - 1)]
    for device in near:
        pl.semaphore_signal(barrier, inc=1, device_id=device, device_id_type=MESH)

    local_copies = [
        pltpu.make_async_copy(src, dst, lsem.at[k])
        for k, (src, dst) in enumerate((
            (fields, field_v), (stem_out, wbuf.at[0]), (stem_in, sbuf.at[0]), (ids_hbm, ids),
            (table_hbm, table), (query_hbm, query), (kvw_hbm, kvw), (regions_hbm, regions),
            (outw_hbm, outw),
        ))
    ]
    for copy in local_copies:
        copy.start()

    pl.semaphore_wait(barrier, len(near))

    def piece_copy(src, s, u, j, send, target):
        at = pl.ds(*PIECES[j])
        return pltpu.make_async_remote_copy(
            src_ref=src.at[u, at, :], dst_ref=wbuf.at[s, u, at, :],
            send_sem=send, recv_sem=wr.at[s, u, j], device_id=target, device_id_type=MESH,
        )

    def whole_copy(u, send):
        return pltpu.make_async_remote_copy(
            src_ref=stem_out.at[u], dst_ref=wbuf.at[1, u], send_sem=send,
            recv_sem=wr.at[1, u, 0], device_id=core_dev, device_id_type=MESH,
        )

    def pixel_copy(k, source, target):
        return pltpu.make_async_remote_copy(
            src_ref=pown.at[source], dst_ref=pbuf.at[k + 1], send_sem=ps.at[k],
            recv_sem=pr.at[k], device_id=target, device_id_type=MESH,
        )

    def stem_copy(k, target):
        return pltpu.make_async_remote_copy(
            src_ref=stem_in, dst_ref=sbuf.at[k + 1], send_sem=ss.at[k],
            recv_sem=sr.at[k], device_id=target, device_id_type=MESH,
        )

    next_dev = (base + g_y, band_next)
    prev_dev = (base + g_y, band_prev)
    sends = [
        piece_copy(stem_out, 2, odd_x, 0, ws.at[0], next_dev),
        piece_copy(stem_out, 2, odd_x, 1, ws.at[1], prev_dev),
        piece_copy(stem_out, 2, odd_x, 2, ws.at[2], next_dev),
        piece_copy(stem_out, 2, odd_x, 3, ws.at[3], prev_dev),
        whole_copy(0, ws.at[10]),
        stem_copy(0, core_dev),
        stem_copy(1, (base + g_y, band_far)),
        stem_copy(2, (base + g_diag, band_far)),
        whole_copy(1, ws.at[11]),
    ]
    later = [
        pixel_copy(0, g_core, core_dev),
        pixel_copy(1, g_y, (base + g_y, bi)),
        pixel_copy(2, g_diag, (base + g_diag, bi)),
        piece_copy(stem_out, 2, odd_x, 4, ws.at[4], next_dev),
        piece_copy(stem_out, 2, odd_x, 5, ws.at[5], prev_dev),
        piece_copy(stem_out, 2, 1 - odd_x, 4, ws.at[6], next_dev),
        piece_copy(stem_out, 2, 1 - odd_x, 5, ws.at[7], prev_dev),
    ]
    for copy in sends:
        copy.start()
    local_copies[0].wait()
    ff = field_v[...].astype(F32).reshape(2, NZ, GROUP, 8, 128)
    for k in range(GROUP):
        pown[k] = ff[:, :, k].reshape(2 * NZ * 8, 128).astype(BF16)
    for copy in later:
        copy.start()
    sends = sends + later
    pbuf[0] = pown[g]

    def forward_x(j, target):
        return piece_copy(wbuf.at[2], 2, odd_x, j, xs.at[j], target)

    def forward_core(u, j):
        at = pl.ds(*PIECES[j])
        return pltpu.make_async_remote_copy(
            src_ref=wbuf.at[2, u, at, :], dst_ref=wbuf.at[3, u, at, :],
            send_sem=fs.at[u, j], recv_sem=wr.at[3, u, j], device_id=core_dev, device_id_type=MESH,
        )

    def arrived(s, u, j):
        piece_copy(stem_out, s, u, j, ws.at[0], core_dev).wait_recv()

    def take_rest(u, pieces):
        for j in pieces:
            forward_core(u, j).start()

    tile[...] = (
        (div(iota((512, 128), 0), 128) == div(iota((512, 128), 1), 4))
        & (mod(iota((512, 128), 0), 4) == mod(iota((512, 128), 1), 4))
    ).astype(F32).astype(BF16)
    for l in range(LATENT):
        lane = iota((128, 1024), 1)
        want = div(mod(lane, WIDTH), HEAD) + l * HEADS + div(lane, WIDTH) * 64
        ex[l] = (iota((128, 1024), 0) == want).astype(F32).astype(BF16)
    for copy in local_copies[3:5]:
        copy.wait()
    onehot = (iota((128, 64), 0) == ids[...]).astype(F32)
    emb[...] = dot(onehot.T.astype(BF16), table[...])
    for copy in local_copies[5:8]:
        copy.wait()
    qf = query[...].astype(F32)
    heads = iota((HEADS, WIDTH), 0) == div(iota((HEADS, WIDTH), 1), HEAD)
    qmat = jnp.concatenate(
        [jnp.where(heads, jnp.broadcast_to(qf[l:l + 1], (HEADS, WIDTH)), 0.0) for l in range(LATENT)],
        axis=0,
    ).astype(BF16)
    folded = dot_nt(qmat, kvw[:, :WIDTH]) * (LOG2E / HEAD**0.5)
    high = folded.astype(BF16).astype(F32)
    qk[...] = jnp.concatenate([high, folded - high], axis=0).T.astype(BF16)

    ones = jnp.ones((128, 128), F32)
    same_tile = div(iota((128, 128), 0), 16) == div(iota((128, 128), 1), 16)
    slot_row = iota((128, 128), 0)
    tile_lane = div(iota((128, 128), 1), 16)
    dest = iota((NVAR, 128), 0)
    dest_region = (div(dest, 4) * GROUP + g) * NBAND + mod(dest, 4) * 2 + yhi
    picked = jnp.zeros((NVAR, 128), F32)

    def slots(row):
        across = row.astype(F32) * ones
        below = jnp.where((across.T < across) & same_tile, 0.5, 0.0)
        return jnp.sum(below, axis=0, keepdims=True).astype(I32)

    for k in range(GROUP):
        row = regions[pl.ds(base + k, 1), :]
        hit = (slots(row) == mod(slot_row, 8)) & (div(slot_row, 32) == k) & (
            tile_lane == x * 2 + mod(div(slot_row, 16), 2)
        )
        in_region = (row == dest_region).astype(F32).astype(BF16)
        picked = picked + dot_nt(in_region, jnp.where(hit, 0.5, 0.0).astype(BF16))
    upper = mod(div(iota((NVAR, 128), 1), 8), 2) == 1
    chosen[...] = jnp.concatenate(
        [jnp.where(upper, 0.0, picked), jnp.where(upper, picked, 0.0)], axis=0
    ).astype(BF16)
    own_row = regions[pl.ds(vi, 1), :]
    own_hit = (slots(own_row) == iota((8, 128), 0)) & (div(iota((8, 128), 1), 16) == bi)
    cell = div(mod(iota((128, CHUNK), 1), HALF), 2)
    average = jnp.where(mod(iota((128, CHUNK), 0), 16) == cell, 0.25, 0.0).astype(BF16)
    pair_mean = dot(own_hit.astype(F32).astype(BF16), average).astype(BF16)
    region = vi * NBAND + bi
    count = jnp.sum((regions[...] == region).astype(F32))

    local_copies[1].wait()
    local_copies[2].wait()
    patch_mask = div(iota((HALF, 128), 1), 4) == iota((HALF, 128), 0)

    def which(t):
        late = div(t, 4)
        second = div(t, 6)
        return (
            (1 - late) * div(t, 2) + late * (2 + mod(t, 2)),
            (1 - late) * mod(t, 2) + late * (odd_x + second - 2 * odd_x * second),
        )

    def first_matrix(t):
        s, u = which(t)
        for k in range(3):
            @pl.when(t == (2, 4, 5)[k])
            def _():
                pixel_copy(k, 0, core_dev).wait_recv()
                stem_copy(k, core_dev).wait_recv()

        fscr[...] = pbuf[s, pl.ds(pl.multiple_of(u * CHUNK, CHUNK), CHUNK), :].astype(F32)
        for a in range(16):
            for i in range(4):
                row = jnp.broadcast_to(fscr[pl.ds(a * 4 + i, 1), :], (HALF, 128))
                lhs[pl.ds(a * HALF, HALF), pl.ds(i * 128, 128)] = jnp.where(
                    patch_mask, row, 0.0
                ).astype(BF16)
        pixels = dot(lhs[...], tile[...]).astype(BF16)[:, :16]
        h = dot(pixels, sbuf[s, u])
        stem = 0.5 * h * (1.0 + jnp.tanh(0.7978845608028654 * (h + 0.044715 * (h * h * h))))
        normed[t] = stem.astype(BF16)

    def second_matrix(t):
        s, u = which(t)

        @pl.when(t == 2)
        def _():
            whole_copy(0, ws.at[0]).wait_recv()

        @pl.when(t == 3)
        def _():
            for j in range(4):
                arrived(2, odd_x, j)
                forward_x(j, (right, left)[j % 2]).start()
            take_rest(odd_x, range(4))
            whole_copy(1, ws.at[0]).wait_recv()

        @pl.when(t == 4)
        def _():
            for j in (4, 5):
                arrived(2, odd_x, j)
            take_rest(odd_x, (4, 5))

        @pl.when(t == 6)
        def _():
            for j in range(6):
                arrived(2, 1 - odd_x, j)
                forward_core(1 - odd_x, j).start()

        @pl.when((t == 5) | (t == 7))
        def _():
            for j in range(6):
                arrived(3, u, j)

        tokens = dot(normed[t], wbuf[s, u]).astype(BF16).astype(F32)
        src_g = mod(s, 2)
        src_core = core + src_g - 2 * core * src_g
        up = div(s, 2)
        src_y = ylo + up - 2 * ylo * up
        var = (base + src_y * 2 + src_core) * 2 + u
        keyed = tokens + emb[pl.ds(var, 1), :]
        centre = jnp.mean(keyed, axis=-1, keepdims=True)
        away = keyed - centre
        spread = jnp.mean(away * away, axis=-1, keepdims=True)
        normed[t] = (away * lax.rsqrt(spread + 1e-05)).astype(BF16)

    def one_variable(t, carry):
        @pl.when(t < 8)
        def _():
            first_matrix(t)

        @pl.when(t > 0)
        def _():
            second_matrix(t - 1)

        return carry

    lax.fori_loop(0, 9, one_variable, 0)

    low_lanes = iota((CHUNK, 128), 1) < 64

    def ring_copies(dr, d, half):
        off = mod(d + dr * (8 - 2 * d), 8)
        target = (mod(z + 1 + 6 * dr, NZ) * GROUP + g, bi)
        start = pl.multiple_of(half * HALF, HALF)
        return (
            pltpu.make_async_remote_copy(
                src_ref=ms.at[off, pl.ds(start, HALF), :], dst_ref=rms.at[dr, d - 1, half],
                send_sem=mss.at[dr, d - 1, half], recv_sem=msr.at[dr, d - 1, half],
                device_id=target, device_id_type=MESH,
            ),
            pltpu.make_async_remote_copy(
                src_ref=part.at[off, pl.ds(start, HALF), :], dst_ref=rpart.at[dr, d - 1, half],
                send_sem=os.at[dr, d - 1, half], recv_sem=orr.at[dr, d - 1, half],
                device_id=target, device_id_type=MESH,
            ),
        )

    def ring_send(dr, d, half):
        for copy in ring_copies(dr, d, half):
            copy.start()

    def local(off):
        start = pl.multiple_of(mod(z + off, NZ) * CHUNK, CHUNK)
        nb = normed[:, pl.ds(start, CHUNK), :].reshape(8 * CHUNK, WIDTH)
        scores = dot(nb, qk[...])
        scores = (scores + pltpu.roll(scores, 64, 1)).reshape(8, CHUNK, 128)
        top = jnp.ceil(jnp.max(scores, axis=0))
        p = jnp.exp2(scores - top[None])
        ms[off] = jnp.where(low_lanes, top, jnp.sum(p, axis=0))
        pb = p.astype(BF16).reshape(8 * CHUNK, 128)
        values = dot(nb, kvw[:, WIDTH:])
        for l in range(LATENT):
            wide = dot(pb, ex[l, :, :WIDTH])
            part[off, :, l * WIDTH:(l + 1) * WIDTH] = jnp.sum(
                (wide * values).reshape(8, CHUNK, WIDTH), axis=0
            ).astype(BF16)

    def offset(dr, d):
        return mod(d + dr * (8 - 2 * d), 8)

    def incoming(d, i):
        for dr, h in ((0, 1 - i), (1, i)):
            for copy in ring_copies(dr, d + 1, h):
                copy.wait_recv()
        parts = []
        for dr, h in ((0, 1 - i), (1, i)):
            parts.append((dr, h, offset(dr, d), pl.ds(pl.multiple_of(h * HALF, HALF), HALF)))
        mine = jnp.concatenate([ms[off, at, :] for _, _, off, at in parts], axis=0)
        other = jnp.concatenate([rms[dr, d, h] for dr, h, _, _ in parts], axis=0)
        mine_r = pltpu.roll(mine, 64, 1)
        other_r = pltpu.roll(other, 64, 1)
        m1 = jnp.where(low_lanes, mine, mine_r)
        s1 = jnp.where(low_lanes, mine_r, mine)
        m2 = jnp.where(low_lanes, other, other_r)
        s2 = jnp.where(low_lanes, other_r, other)
        m = jnp.maximum(m1, m2)
        a1 = jnp.exp2(m1 - m)
        a2 = jnp.exp2(m2 - m)
        return parts, m, a1, a2, a1 * s1 + a2 * s2

    def merge(d, i):
        parts, m, a1, a2, s = incoming(d, i)
        new = jnp.where(low_lanes, m, s)
        ab = jnp.where(low_lanes, a2, a1).astype(BF16)
        for k, (_, _, off, at) in enumerate(parts):
            ms[off, at, :] = new[k * HALF:(k + 1) * HALF]
        for l in range(LATENT):
            cols = slice(l * WIDTH, (l + 1) * WIDTH)
            factor = dot(ab, ex[l])
            for k, (dr, h, off, at) in enumerate(parts):
                lines = slice(k * HALF, (k + 1) * HALF)
                part[off, at, cols] = (
                    factor[lines, :WIDTH] * rpart[dr, d, h, :, cols].astype(F32)
                    + factor[lines, WIDTH:] * part[off, at, cols].astype(F32)
                ).astype(BF16)

    def one_chunk(k, carry):
        odd = mod(k, 2)
        d = 3 - div(k - 2, 2)
        i = mod(k, 2)

        @pl.when(k < 8)
        def _():
            local(4 - div(k + 1, 2) * odd + div(k, 2) * (1 - odd))

        @pl.when(k == 0)
        def _():
            ring_send(0, 4, 0)
            ring_send(1, 4, 1)

        @pl.when(k > 2)
        def _():
            merge(d, i)

        @pl.when((k > 1) & (k < 8))
        def _():
            ring_send(0, d, 1 - i)
            ring_send(1, d, i)

        return carry

    lax.fori_loop(0, 9, one_chunk, 0)

    parts, _, a1, a2, s = incoming(0, 1)
    weight = jnp.where(low_lanes, a2, a1) / s
    weight_high = weight.astype(BF16).astype(F32)
    ab = jnp.concatenate([weight_high, weight - weight_high], axis=0).astype(BF16)
    mixed = []
    for l in range(LATENT):
        cols = slice(l * WIDTH, (l + 1) * WIDTH)
        factor = dot(ab, ex[l])
        factor = factor[:CHUNK] + factor[CHUNK:]
        received = jnp.concatenate([rpart[0, 0, 0, :, cols], rpart[1, 0, 1, :, cols]], axis=0)
        mixed.append(
            (factor[:, :WIDTH] * received.astype(F32)
             + factor[:, WIDTH:] * part[0, :, cols].astype(F32)).astype(BF16)
        )
    local_copies[8].wait()
    projected = dot(jnp.concatenate(mixed, axis=0), outw[...])
    sums = []
    for l in range(LATENT):
        cols = slice(l * WIDTH, (l + 1) * WIDTH)
        out = (projected[l * CHUNK:(l + 1) * CHUNK] + qf[l:l + 1]).astype(BF16)
        lat[:, cols] = out
        sums.append(dot(pair_mean, out))
    pairs[member] = jnp.concatenate(
        [jnp.concatenate(sums[:2], axis=1), jnp.concatenate(sums[2:], axis=1)], axis=0
    ).astype(BF16)

    def pair_copy(j, slot):
        return pltpu.make_async_remote_copy(
            src_ref=pairs.at[slot], dst_ref=pairs.at[slot], send_sem=cs.at[j], recv_sem=cr.at[j],
            device_id=member_dev(j), device_id_type=MESH,
        )

    order = (1, 3, 5, 4, 7, 6, 2)
    for j in order:
        pair_copy(j, member).start()
    for j in order:
        other = (flip(ylo, j // 4) * 2 + flip(core, (j // 2) % 2)) * 2 + flip(yhi, j % 2)
        pair_copy(j, other).wait_recv()
    by_dest = dot(chosen[...], pairs[...].reshape(128, 2 * WIDTH))
    for k in range(16):
        table_f[:, k, :] = by_dest[(k // 8) * NVAR:(k // 8 + 1) * NVAR, (k % 8) * 128:(k % 8 + 1) * 128]
    table_b[...] = table_f[...].astype(BF16)

    def row_copy(i):
        to_z, to_x = place_off(i)
        return pltpu.make_async_remote_copy(
            src_ref=table_b.at[to_z * 4 + to_x], dst_ref=rows.at[i], send_sem=ts.at[i],
            recv_sem=tr.at[i], device_id=(to_z * GROUP + g, to_x * 2 + yhi), device_id_type=MESH,
        )

    def row_send(j, carry):
        row_copy(j).start()
        return carry

    def row_wait(j, carry):
        row_copy(j).wait_recv()
        return carry

    lax.fori_loop(0, NVAR - 1, row_send, 0)
    rows[NVAR - 1] = table_b[z * 4 + x]
    for copy in sends:
        copy.wait_send()
    for j in range(4):
        forward_x(j, (right, left)[j % 2]).wait_send()
    for j in range(6):
        forward_core(0, j).wait_send()
        forward_core(1, j).wait_send()

    def ring_over(i, carry):
        dr = mod(i, 2)
        half = mod(div(i, 2), 2)
        d = 1 + div(i, 4)

        @pl.when((d < 4) | (half == dr))
        def _():
            for copy in ring_copies(dr, d, half):
                copy.wait_send()

        return carry

    for j in order:
        pair_copy(j, member).wait_send()

    def row_over(j, carry):
        row_copy(j).wait_send()
        return carry

    lax.fori_loop(0, 16, ring_over, 0)
    lax.fori_loop(0, NVAR - 1, row_over, 0)
    lax.fori_loop(0, NVAR - 1, row_wait, 0)
    total = jnp.sum(rows[...].astype(F32), axis=0) / count
    for l in range(LATENT):
        for k in range(4):
            means[0, l:l + 1, k * 128:(k + 1) * 128] = total[l * 4 + k:l * 4 + k + 1, :]


def shards(fields, stem_in, stem_out, level_ids, level_table, latent_query, kv_weight, out_weight, region_ids):
    vmem = pl.BlockSpec(memory_space=pltpu.VMEM)
    dma = pltpu.SemaphoreType.DMA
    lat, means = pl.pallas_call(
        kernel,
        out_shape=(
            jax.ShapeDtypeStruct((CHUNK, FLAT), BF16),
            jax.ShapeDtypeStruct((1, LATENT, WIDTH), F32),
        ),
        in_specs=[pl.BlockSpec(memory_space=pl.ANY)] * 9,
        out_specs=(vmem, vmem),
        scratch_shapes=[
            pltpu.VMEM((2, 256, 128), BF16),
            pltpu.VMEM((1, 64), I32),
            pltpu.VMEM((128, WIDTH), BF16),
            pltpu.VMEM((LATENT, WIDTH), BF16),
            pltpu.VMEM((WIDTH, 2 * WIDTH), BF16),
            pltpu.VMEM((WIDTH, WIDTH), BF16),
            pltpu.VMEM((32, 128), I32),
            pltpu.VMEM((GROUP, 128, 128), BF16),
            pltpu.VMEM((GROUP, 128, 128), BF16),
            pltpu.VMEM((GROUP, 2, 16, WIDTH), BF16),
            pltpu.VMEM((GROUP, 2, WIDTH, WIDTH), BF16),
            pltpu.VMEM((CHUNK, 128), F32),
            pltpu.VMEM((512, 512), BF16),
            pltpu.VMEM((512, 128), BF16),
            pltpu.VMEM((8, 512, WIDTH), BF16),
            pltpu.VMEM((64, WIDTH), F32),
            pltpu.VMEM((WIDTH, 128), BF16),
            pltpu.VMEM((LATENT, 128, 2 * WIDTH), BF16),
            pltpu.VMEM((NZ, CHUNK, FLAT), BF16),
            pltpu.VMEM((NZ, CHUNK, 128), F32),
            pltpu.VMEM((2, 4, 2, HALF, FLAT), BF16),
            pltpu.VMEM((2, 4, 2, HALF, 128), F32),
            pltpu.VMEM((2 * NVAR, 128), BF16),
            pltpu.VMEM((8, 16, 2 * WIDTH), BF16),
            pltpu.VMEM((NVAR, 16, 128), F32),
            pltpu.VMEM((NVAR, 16, 128), BF16),
            pltpu.VMEM((NVAR, 16, 128), BF16),
            dma((9,)),
            dma((3,)), dma((3,)),
            dma((3,)), dma((3,)),
            dma((12,)), dma((GROUP, 2, 6)), dma((4,)), dma((2, 6)),
            dma((2, 4, 2)), dma((2, 4, 2)),
            dma((2, 4, 2)), dma((2, 4, 2)),
            dma((8,)), dma((8,)),
            dma((NVAR,)), dma((NVAR,)),
        ],
        compiler_params=pltpu.CompilerParams(
            collective_id=0, has_side_effects=True, vmem_limit_bytes=60 * 1024 * 1024
        ),
        name="window",
    )(
        fields, stem_in, stem_out, level_ids.reshape(1, -1), level_table, latent_query,
        kv_weight, out_weight, region_ids,
    )
    return lat.reshape(2, 32, LATENT, WIDTH), means


def solution(mesh):
    in_specs = (
        P("var", None, "band"),
        P("var", None, None),
        P("var", None, None),
        P(),
        P(),
        P(),
        P(),
        P(),
        P(),
    )
    out_specs = (P("var", "band", None, None), P(("var", "band"), None, None))
    return jax.shard_map(shards, mesh=mesh, in_specs=in_specs, out_specs=out_specs, check_vma=False)
```

```python
import jax
import jax.numpy as jnp
from jax import lax
from jax.experimental import pallas as pl
from jax.experimental.pallas import tpu as pltpu
from jax.sharding import PartitionSpec as P

MESH = pl.DeviceIdType.MESH
BF16 = jnp.bfloat16
F32 = jnp.float32
I32 = jnp.int32

HEADS = 16
HEAD = 32
WIDTH = 512
LATENT = 4
FLAT = LATENT * WIDTH
NZ = 8
GROUP = 4
NVAR = 32
NBAND = 8
CHUNK = 64
HALF = 32
LOG2E = 1.4426950408889634
PIECES = ((0, 128), (128, 128), (256, 128), (384, 128))


def iota(shape, axis):
    return lax.broadcasted_iota(I32, shape, axis)


def dot(a, b):
    return jnp.dot(a, b, preferred_element_type=F32)


def dot_nt(a, b):
    return lax.dot_general(a, b, (((1,), (1,)), ((), ())), preferred_element_type=F32)


def mod(a, n):
    return lax.rem(a, jnp.int32(n))


def div(a, n):
    return lax.div(a, jnp.int32(n))


def kernel(
    fields, stem_in, stem_out, ids_hbm, table_hbm, query_hbm, kvw_hbm, outw_hbm, regions_hbm,
    lat, means,
    field_v, ids, table, query, kvw, outw, regions,
    pbuf, pown, sbuf, wbuf, fscr, lhs, tile, normed, emb, qk, ex,
    part, ms, rpart, rms, chosen, pairs, table_f, table_b, rows,
    lsem, ps, pr, ss, sr, ws, wr, xs, fs, os, orr, mss, msr, cs, cr, ts, tr,
):
    vi = lax.axis_index("var")
    bi = lax.axis_index("band")
    z = div(vi, GROUP)
    g = mod(vi, GROUP)
    ylo = div(g, 2)
    core = mod(g, 2)
    x = div(bi, 2)
    yhi = mod(bi, 2)
    y = yhi * 2 + ylo
    odd_x = mod(x, 2)
    base = z * GROUP
    g_core = ylo * 2 + 1 - core
    g_y = (1 - ylo) * 2 + core
    g_diag = (1 - ylo) * 2 + 1 - core
    core_dev = (base + g_core, bi)
    band_next = x * 2 + div(mod(y + 1, 4), 2)
    band_prev = x * 2 + div(mod(y + 3, 4), 2)
    band_far = x * 2 + 1 - yhi
    right = (vi, mod(x + 1, 4) * 2 + yhi)
    left = (vi, mod(x + 3, 4) * 2 + yhi)
    member = g * 2 + yhi

    def flip(bit, by):
        return mod(bit + by, 2)

    def member_dev(j):
        other = flip(ylo, j // 4) * 2 + flip(core, (j // 2) % 2)
        return (base + other, x * 2 + flip(yhi, j % 2))

    def place_off(i):
        a, b = div(i, 4), mod(i, 4)
        da = 4 - div(a + 1, 2) * mod(a, 2) + div(a, 2) * (1 - mod(a, 2))
        db = 2 - div(b + 1, 2) * mod(b, 2) + div(b, 2) * (1 - mod(b, 2))
        return mod(z + da, NZ), mod(x + db, 4)

    barrier = pltpu.get_barrier_semaphore()
    near = [member_dev(j) for j in range(1, 8)]
    near += [(vi, mod(x + j, 4) * 2 + yhi) for j in range(1, 4)]
    near += [(mod(z + j, NZ) * GROUP + g, bi) for j in (1, NZ - 1)]
    for device in near:
        pl.semaphore_signal(barrier, inc=1, device_id=device, device_id_type=MESH)

    local_copies = [
        pltpu.make_async_copy(src, dst, lsem.at[k])
        for k, (src, dst) in enumerate((
            (fields, field_v), (stem_out, wbuf.at[0]), (stem_in, sbuf.at[0]), (ids_hbm, ids),
            (table_hbm, table), (query_hbm, query), (kvw_hbm, kvw), (regions_hbm, regions),
            (outw_hbm, outw),
        ))
    ]
    for copy in local_copies:
        copy.start()

    pl.semaphore_wait(barrier, len(near))

    def piece_copy(src, s, u, j, send, target):
        at = pl.ds(*PIECES[j])
        return pltpu.make_async_remote_copy(
            src_ref=src.at[u, at, :], dst_ref=wbuf.at[s, u, at, :],
            send_sem=send, recv_sem=wr.at[s, u, j], device_id=target, device_id_type=MESH,
        )

    def whole_copy(u, send):
        return pltpu.make_async_remote_copy(
            src_ref=stem_out.at[u], dst_ref=wbuf.at[1, u], send_sem=send,
            recv_sem=wr.at[1, u, 0], device_id=core_dev, device_id_type=MESH,
        )

    def pixel_copy(k, source, target):
        return pltpu.make_async_remote_copy(
            src_ref=pown.at[source], dst_ref=pbuf.at[k + 1], send_sem=ps.at[k],
            recv_sem=pr.at[k], device_id=target, device_id_type=MESH,
        )

    def stem_copy(k, target):
        return pltpu.make_async_remote_copy(
            src_ref=stem_in, dst_ref=sbuf.at[k + 1], send_sem=ss.at[k],
            recv_sem=sr.at[k], device_id=target, device_id_type=MESH,
        )

    next_dev = (base + g_y, band_next)
    prev_dev = (base + g_y, band_prev)
    sends = [
        piece_copy(stem_out, 2, odd_x, 0, ws.at[0], next_dev),
        piece_copy(stem_out, 2, odd_x, 1, ws.at[1], prev_dev),
        whole_copy(0, ws.at[6]),
        stem_copy(0, core_dev),
        stem_copy(1, (base + g_y, band_far)),
        stem_copy(2, (base + g_diag, band_far)),
        whole_copy(1, ws.at[7]),
    ]
    later = [
        pixel_copy(0, g_core, core_dev),
        pixel_copy(1, g_y, (base + g_y, bi)),
        pixel_copy(2, g_diag, (base + g_diag, bi)),
    ]
    for copy in sends:
        copy.start()
    local_copies[0].wait()
    ff = field_v[...].astype(F32).reshape(2, NZ, GROUP, 8, 128)
    for k in range(GROUP):
        pown[k] = ff[:, :, k].reshape(2 * NZ * 8, 128).astype(BF16)
    for copy in later:
        copy.start()
    held = [
        piece_copy(stem_out, 2, odd_x, 2, ws.at[2], next_dev),
        piece_copy(stem_out, 2, odd_x, 3, ws.at[3], prev_dev),
        piece_copy(stem_out, 2, 1 - odd_x, 2, ws.at[4], next_dev),
        piece_copy(stem_out, 2, 1 - odd_x, 3, ws.at[5], prev_dev),
    ]
    sends = sends + later + held
    pbuf[0] = pown[g]

    def forward_x(j, target):
        return piece_copy(wbuf.at[2], 2, odd_x, j, xs.at[j], target)

    def forward_core(u, j):
        at = pl.ds(*PIECES[j])
        return pltpu.make_async_remote_copy(
            src_ref=wbuf.at[2, u, at, :], dst_ref=wbuf.at[3, u, at, :],
            send_sem=fs.at[u, j], recv_sem=wr.at[3, u, j], device_id=core_dev, device_id_type=MESH,
        )

    def arrived(s, u, j):
        piece_copy(stem_out, s, u, j, ws.at[0], core_dev).wait_recv()

    def take_rest(u, pieces):
        for j in pieces:
            forward_core(u, j).start()

    tile[...] = (
        (div(iota((512, 128), 0), 128) == div(iota((512, 128), 1), 4))
        & (mod(iota((512, 128), 0), 4) == mod(iota((512, 128), 1), 4))
    ).astype(F32).astype(BF16)
    for l in range(LATENT):
        lane = iota((128, 1024), 1)
        want = div(mod(lane, WIDTH), HEAD) + l * HEADS + div(lane, WIDTH) * 64
        ex[l] = (iota((128, 1024), 0) == want).astype(F32).astype(BF16)
    for copy in local_copies[3:5]:
        copy.wait()
    onehot = (iota((128, 64), 0) == ids[...]).astype(F32)
    emb[...] = dot(onehot.T.astype(BF16), table[...])
    for copy in local_copies[5:8]:
        copy.wait()
    qf = query[...].astype(F32)
    heads = iota((HEADS, WIDTH), 0) == div(iota((HEADS, WIDTH), 1), HEAD)
    qmat = jnp.concatenate(
        [jnp.where(heads, jnp.broadcast_to(qf[l:l + 1], (HEADS, WIDTH)), 0.0) for l in range(LATENT)],
        axis=0,
    ).astype(BF16)
    folded = dot_nt(qmat, kvw[:, :WIDTH]) * (LOG2E / HEAD**0.5)
    high = folded.astype(BF16).astype(F32)
    qk[...] = jnp.concatenate([high, folded - high], axis=0).T.astype(BF16)

    ones = jnp.ones((128, 128), F32)
    same_tile = div(iota((128, 128), 0), 16) == div(iota((128, 128), 1), 16)
    slot_row = iota((128, 128), 0)
    tile_lane = div(iota((128, 128), 1), 16)
    dest = iota((NVAR, 128), 0)
    dest_region = (div(dest, 4) * GROUP + g) * NBAND + mod(dest, 4) * 2 + yhi
    picked = jnp.zeros((NVAR, 128), F32)

    def slots(row):
        across = row.astype(F32) * ones
        below = jnp.where((across.T < across) & same_tile, 0.5, 0.0)
        return jnp.sum(below, axis=0, keepdims=True).astype(I32)

    for k in range(GROUP):
        row = regions[pl.ds(base + k, 1), :]
        hit = (slots(row) == mod(slot_row, 8)) & (div(slot_row, 32) == k) & (
            tile_lane == x * 2 + mod(div(slot_row, 16), 2)
        )
        in_region = (row == dest_region).astype(F32).astype(BF16)
        picked = picked + dot_nt(in_region, jnp.where(hit, 0.5, 0.0).astype(BF16))
    upper = mod(div(iota((NVAR, 128), 1), 8), 2) == 1
    chosen[...] = jnp.concatenate(
        [jnp.where(upper, 0.0, picked), jnp.where(upper, picked, 0.0)], axis=0
    ).astype(BF16)
    own_row = regions[pl.ds(vi, 1), :]
    own_hit = (slots(own_row) == iota((8, 128), 0)) & (div(iota((8, 128), 1), 16) == bi)
    cell = div(mod(iota((128, CHUNK), 1), HALF), 2)
    average = jnp.where(mod(iota((128, CHUNK), 0), 16) == cell, 0.25, 0.0).astype(BF16)
    pair_mean = dot(own_hit.astype(F32).astype(BF16), average).astype(BF16)
    region = vi * NBAND + bi
    count = jnp.sum((regions[...] == region).astype(F32))

    local_copies[1].wait()
    local_copies[2].wait()
    patch_mask = div(iota((HALF, 128), 1), 4) == iota((HALF, 128), 0)

    def which(t):
        late = div(t, 4)
        second = div(t, 6)
        return (
            (1 - late) * div(t, 2) + late * (2 + mod(t, 2)),
            (1 - late) * mod(t, 2) + late * (odd_x + second - 2 * odd_x * second),
        )

    def first_matrix(t):
        s, u = which(t)
        for k in range(3):
            @pl.when(t == (2, 4, 5)[k])
            def _():
                pixel_copy(k, 0, core_dev).wait_recv()
                stem_copy(k, core_dev).wait_recv()

        fscr[...] = pbuf[s, pl.ds(pl.multiple_of(u * CHUNK, CHUNK), CHUNK), :].astype(F32)
        for a in range(16):
            for i in range(4):
                row = jnp.broadcast_to(fscr[pl.ds(a * 4 + i, 1), :], (HALF, 128))
                lhs[pl.ds(a * HALF, HALF), pl.ds(i * 128, 128)] = jnp.where(
                    patch_mask, row, 0.0
                ).astype(BF16)
        pixels = dot(lhs[...], tile[...]).astype(BF16)[:, :16]
        h = dot(pixels, sbuf[s, u])
        stem = 0.5 * h * (1.0 + jnp.tanh(0.7978845608028654 * (h + 0.044715 * (h * h * h))))
        normed[t] = stem.astype(BF16)

    def second_matrix(t):
        s, u = which(t)

        @pl.when(t == 1)
        def _():
            for copy in held[:2]:
                copy.start()

        @pl.when(t == 2)
        def _():
            whole_copy(0, ws.at[0]).wait_recv()

        @pl.when(t == 3)
        def _():
            for j in range(2):
                arrived(2, odd_x, j)
                forward_x(j, (right, left)[j]).start()
            for copy in held[2:]:
                copy.start()
            take_rest(odd_x, range(2))
            whole_copy(1, ws.at[0]).wait_recv()

        @pl.when(t == 4)
        def _():
            for j in (2, 3):
                arrived(2, odd_x, j)
            take_rest(odd_x, (2, 3))

        @pl.when(t == 6)
        def _():
            for j in range(4):
                arrived(2, 1 - odd_x, j)
                forward_core(1 - odd_x, j).start()

        @pl.when((t == 5) | (t == 7))
        def _():
            for j in range(4):
                arrived(3, u, j)

        tokens = dot(normed[t], wbuf[s, u]).astype(BF16).astype(F32)
        src_g = mod(s, 2)
        src_core = core + src_g - 2 * core * src_g
        up = div(s, 2)
        src_y = ylo + up - 2 * ylo * up
        var = (base + src_y * 2 + src_core) * 2 + u
        keyed = tokens + emb[pl.ds(var, 1), :]
        centre = jnp.mean(keyed, axis=-1, keepdims=True)
        away = keyed - centre
        spread = jnp.mean(away * away, axis=-1, keepdims=True)
        normed[t] = (away * lax.rsqrt(spread + 1e-05)).astype(BF16)

    def one_variable(t, carry):
        @pl.when(t < 8)
        def _():
            first_matrix(t)

        @pl.when(t > 0)
        def _():
            second_matrix(t - 1)

        return carry

    lax.fori_loop(0, 9, one_variable, 0)

    low_lanes = iota((CHUNK, 128), 1) < 64

    def ring_copies(dr, d, half):
        off = mod(d + dr * (8 - 2 * d), 8)
        target = (mod(z + 1 + 6 * dr, NZ) * GROUP + g, bi)
        start = pl.multiple_of(half * HALF, HALF)
        return (
            pltpu.make_async_remote_copy(
                src_ref=ms.at[off, pl.ds(start, HALF), :], dst_ref=rms.at[dr, d - 1, half],
                send_sem=mss.at[dr, d - 1, half], recv_sem=msr.at[dr, d - 1, half],
                device_id=target, device_id_type=MESH,
            ),
            pltpu.make_async_remote_copy(
                src_ref=part.at[off, pl.ds(start, HALF), :], dst_ref=rpart.at[dr, d - 1, half],
                send_sem=os.at[dr, d - 1, half], recv_sem=orr.at[dr, d - 1, half],
                device_id=target, device_id_type=MESH,
            ),
        )

    def ring_send(dr, d, half):
        for copy in ring_copies(dr, d, half):
            copy.start()

    def local(off):
        start = pl.multiple_of(mod(z + off, NZ) * CHUNK, CHUNK)
        nb = normed[:, pl.ds(start, CHUNK), :].reshape(8 * CHUNK, WIDTH)
        scores = dot(nb, qk[...])
        scores = (scores + pltpu.roll(scores, 64, 1)).reshape(8, CHUNK, 128)
        top = jnp.ceil(jnp.max(scores, axis=0))
        p = jnp.exp2(scores - top[None])
        ms[off] = jnp.where(low_lanes, top, jnp.sum(p, axis=0))
        pb = p.astype(BF16).reshape(8 * CHUNK, 128)
        values = dot(nb, kvw[:, WIDTH:])
        for l in range(LATENT):
            wide = dot(pb, ex[l, :, :WIDTH])
            part[off, :, l * WIDTH:(l + 1) * WIDTH] = jnp.sum(
                (wide * values).reshape(8, CHUNK, WIDTH), axis=0
            ).astype(BF16)

    def offset(dr, d):
        return mod(d + dr * (8 - 2 * d), 8)

    def incoming(d, i):
        for dr, h in ((0, 1 - i), (1, i)):
            for copy in ring_copies(dr, d + 1, h):
                copy.wait_recv()
        parts = []
        for dr, h in ((0, 1 - i), (1, i)):
            parts.append((dr, h, offset(dr, d), pl.ds(pl.multiple_of(h * HALF, HALF), HALF)))
        mine = jnp.concatenate([ms[off, at, :] for _, _, off, at in parts], axis=0)
        other = jnp.concatenate([rms[dr, d, h] for dr, h, _, _ in parts], axis=0)
        mine_r = pltpu.roll(mine, 64, 1)
        other_r = pltpu.roll(other, 64, 1)
        m1 = jnp.where(low_lanes, mine, mine_r)
        s1 = jnp.where(low_lanes, mine_r, mine)
        m2 = jnp.where(low_lanes, other, other_r)
        s2 = jnp.where(low_lanes, other_r, other)
        m = jnp.maximum(m1, m2)
        a1 = jnp.exp2(m1 - m)
        a2 = jnp.exp2(m2 - m)
        return parts, m, a1, a2, a1 * s1 + a2 * s2

    def merge(d, i):
        parts, m, a1, a2, s = incoming(d, i)
        new = jnp.where(low_lanes, m, s)
        ab = jnp.where(low_lanes, a2, a1).astype(BF16)
        for k, (_, _, off, at) in enumerate(parts):
            ms[off, at, :] = new[k * HALF:(k + 1) * HALF]
        for l in range(LATENT):
            cols = slice(l * WIDTH, (l + 1) * WIDTH)
            factor = dot(ab, ex[l])
            for k, (dr, h, off, at) in enumerate(parts):
                lines = slice(k * HALF, (k + 1) * HALF)
                part[off, at, cols] = (
                    factor[lines, :WIDTH] * rpart[dr, d, h, :, cols].astype(F32)
                    + factor[lines, WIDTH:] * part[off, at, cols].astype(F32)
                ).astype(BF16)

    def one_chunk(k, carry):
        odd = mod(k, 2)
        d = 3 - div(k - 2, 2)
        i = mod(k, 2)

        @pl.when(k < 8)
        def _():
            local(4 - div(k + 1, 2) * odd + div(k, 2) * (1 - odd))

        @pl.when(k == 0)
        def _():
            ring_send(0, 4, 0)
            ring_send(1, 4, 1)

        @pl.when(k > 2)
        def _():
            merge(d, i)

        @pl.when((k > 1) & (k < 8))
        def _():
            ring_send(0, d, 1 - i)
            ring_send(1, d, i)

        return carry

    lax.fori_loop(0, 9, one_chunk, 0)

    parts, _, a1, a2, s = incoming(0, 1)
    weight = jnp.where(low_lanes, a2, a1) / s
    weight_high = weight.astype(BF16).astype(F32)
    ab = jnp.concatenate([weight_high, weight - weight_high], axis=0).astype(BF16)
    mixed = []
    for l in range(LATENT):
        cols = slice(l * WIDTH, (l + 1) * WIDTH)
        factor = dot(ab, ex[l])
        factor = factor[:CHUNK] + factor[CHUNK:]
        received = jnp.concatenate([rpart[0, 0, 0, :, cols], rpart[1, 0, 1, :, cols]], axis=0)
        mixed.append(
            (factor[:, :WIDTH] * received.astype(F32)
             + factor[:, WIDTH:] * part[0, :, cols].astype(F32)).astype(BF16)
        )
    local_copies[8].wait()
    projected = dot(jnp.concatenate(mixed, axis=0), outw[...])
    sums = []
    for l in range(LATENT):
        cols = slice(l * WIDTH, (l + 1) * WIDTH)
        out = (projected[l * CHUNK:(l + 1) * CHUNK] + qf[l:l + 1]).astype(BF16)
        lat[:, cols] = out
        sums.append(dot(pair_mean, out))
    pairs[member] = jnp.concatenate(
        [jnp.concatenate(sums[:2], axis=1), jnp.concatenate(sums[2:], axis=1)], axis=0
    ).astype(BF16)

    def pair_copy(j, slot):
        return pltpu.make_async_remote_copy(
            src_ref=pairs.at[slot], dst_ref=pairs.at[slot], send_sem=cs.at[j], recv_sem=cr.at[j],
            device_id=member_dev(j), device_id_type=MESH,
        )

    order = (1, 3, 5, 4, 7, 6, 2)
    for j in order:
        pair_copy(j, member).start()
    for j in order:
        other = (flip(ylo, j // 4) * 2 + flip(core, (j // 2) % 2)) * 2 + flip(yhi, j % 2)
        pair_copy(j, other).wait_recv()
    by_dest = dot(chosen[...], pairs[...].reshape(128, 2 * WIDTH))
    for k in range(16):
        table_f[:, k, :] = by_dest[(k // 8) * NVAR:(k // 8 + 1) * NVAR, (k % 8) * 128:(k % 8 + 1) * 128]
    table_b[...] = table_f[...].astype(BF16)

    def row_copy(i):
        to_z, to_x = place_off(i)
        return pltpu.make_async_remote_copy(
            src_ref=table_b.at[to_z * 4 + to_x], dst_ref=rows.at[i], send_sem=ts.at[i],
            recv_sem=tr.at[i], device_id=(to_z * GROUP + g, to_x * 2 + yhi), device_id_type=MESH,
        )

    def row_send(j, carry):
        row_copy(j).start()
        return carry

    def row_wait(j, carry):
        row_copy(j).wait_recv()
        return carry

    lax.fori_loop(0, NVAR - 1, row_send, 0)
    rows[NVAR - 1] = table_b[z * 4 + x]
    for copy in sends:
        copy.wait_send()
    for j in range(2):
        forward_x(j, (right, left)[j]).wait_send()
    for j in range(4):
        forward_core(0, j).wait_send()
        forward_core(1, j).wait_send()

    def ring_over(i, carry):
        dr = mod(i, 2)
        half = mod(div(i, 2), 2)
        d = 1 + div(i, 4)

        @pl.when((d < 4) | (half == dr))
        def _():
            for copy in ring_copies(dr, d, half):
                copy.wait_send()

        return carry

    for j in order:
        pair_copy(j, member).wait_send()

    def row_over(j, carry):
        row_copy(j).wait_send()
        return carry

    lax.fori_loop(0, 16, ring_over, 0)
    lax.fori_loop(0, NVAR - 1, row_over, 0)
    lax.fori_loop(0, NVAR - 1, row_wait, 0)
    total = jnp.sum(rows[...].astype(F32), axis=0) / count
    for l in range(LATENT):
        for k in range(4):
            means[0, l:l + 1, k * 128:(k + 1) * 128] = total[l * 4 + k:l * 4 + k + 1, :]


def shards(fields, stem_in, stem_out, level_ids, level_table, latent_query, kv_weight, out_weight, region_ids):
    vmem = pl.BlockSpec(memory_space=pltpu.VMEM)
    dma = pltpu.SemaphoreType.DMA
    lat, means = pl.pallas_call(
        kernel,
        out_shape=(
            jax.ShapeDtypeStruct((CHUNK, FLAT), BF16),
            jax.ShapeDtypeStruct((1, LATENT, WIDTH), F32),
        ),
        in_specs=[pl.BlockSpec(memory_space=pl.ANY)] * 9,
        out_specs=(vmem, vmem),
        scratch_shapes=[
            pltpu.VMEM((2, 256, 128), BF16),
            pltpu.VMEM((1, 64), I32),
            pltpu.VMEM((128, WIDTH), BF16),
            pltpu.VMEM((LATENT, WIDTH), BF16),
            pltpu.VMEM((WIDTH, 2 * WIDTH), BF16),
            pltpu.VMEM((WIDTH, WIDTH), BF16),
            pltpu.VMEM((32, 128), I32),
            pltpu.VMEM((GROUP, 128, 128), BF16),
            pltpu.VMEM((GROUP, 128, 128), BF16),
            pltpu.VMEM((GROUP, 2, 16, WIDTH), BF16),
            pltpu.VMEM((GROUP, 2, WIDTH, WIDTH), BF16),
            pltpu.VMEM((CHUNK, 128), F32),
            pltpu.VMEM((512, 512), BF16),
            pltpu.VMEM((512, 128), BF16),
            pltpu.VMEM((8, 512, WIDTH), BF16),
            pltpu.VMEM((64, WIDTH), F32),
            pltpu.VMEM((WIDTH, 128), BF16),
            pltpu.VMEM((LATENT, 128, 2 * WIDTH), BF16),
            pltpu.VMEM((NZ, CHUNK, FLAT), BF16),
            pltpu.VMEM((NZ, CHUNK, 128), F32),
            pltpu.VMEM((2, 4, 2, HALF, FLAT), BF16),
            pltpu.VMEM((2, 4, 2, HALF, 128), F32),
            pltpu.VMEM((2 * NVAR, 128), BF16),
            pltpu.VMEM((8, 16, 2 * WIDTH), BF16),
            pltpu.VMEM((NVAR, 16, 128), F32),
            pltpu.VMEM((NVAR, 16, 128), BF16),
            pltpu.VMEM((NVAR, 16, 128), BF16),
            dma((9,)),
            dma((3,)), dma((3,)),
            dma((3,)), dma((3,)),
            dma((8,)), dma((GROUP, 2, 4)), dma((2,)), dma((2, 4)),
            dma((2, 4, 2)), dma((2, 4, 2)),
            dma((2, 4, 2)), dma((2, 4, 2)),
            dma((8,)), dma((8,)),
            dma((NVAR,)), dma((NVAR,)),
        ],
        compiler_params=pltpu.CompilerParams(
            collective_id=0, has_side_effects=True, vmem_limit_bytes=60 * 1024 * 1024
        ),
        name="window",
    )(
        fields, stem_in, stem_out, level_ids.reshape(1, -1), level_table, latent_query,
        kv_weight, out_weight, region_ids,
    )
    return lat.reshape(2, 32, LATENT, WIDTH), means


def solution(mesh):
    in_specs = (
        P("var", None, "band"),
        P("var", None, None),
        P("var", None, None),
        P(),
        P(),
        P(),
        P(),
        P(),
        P(),
    )
    out_specs = (P("var", "band", None, None), P(("var", "band"), None, None))
    return jax.shard_map(shards, mesh=mesh, in_specs=in_specs, out_specs=out_specs, check_vma=False)
```

```python
import jax
import jax.numpy as jnp
from jax import lax
from jax.experimental import pallas as pl
from jax.experimental.pallas import tpu as pltpu
from jax.sharding import PartitionSpec as P

MESH = pl.DeviceIdType.MESH
BF16 = jnp.bfloat16
F32 = jnp.float32
I32 = jnp.int32

HEADS = 16
HEAD = 32
WIDTH = 512
LATENT = 4
FLAT = LATENT * WIDTH
NZ = 8
GROUP = 4
NVAR = 32
NBAND = 8
CHUNK = 64
HALF = 32
LOG2E = 1.4426950408889634
PIECES = ((0, 128), (128, 128), (256, 128), (384, 128))


def iota(shape, axis):
    return lax.broadcasted_iota(I32, shape, axis)


def dot(a, b):
    return jnp.dot(a, b, preferred_element_type=F32)


def dot_nt(a, b):
    return lax.dot_general(a, b, (((1,), (1,)), ((), ())), preferred_element_type=F32)


def mod(a, n):
    return lax.rem(a, jnp.int32(n))


def div(a, n):
    return lax.div(a, jnp.int32(n))


def kernel(
    fields, stem_in, stem_out, ids_hbm, table_hbm, query_hbm, kvw_hbm, outw_hbm, regions_hbm,
    lat, means,
    field_v, ids, table, query, kvw, outw, regions,
    pbuf, pown, sbuf, wbuf, fscr, lhs, tile, normed, emb, qk, ex,
    part, ms, rpart, rms, chosen, pairs, table_f, table_b, rows,
    lsem, ps, pr, ss, sr, ws, wr, xs, fs, os, orr, mss, msr, cs, cr, ts, tr,
):
    vi = lax.axis_index("var")
    bi = lax.axis_index("band")
    z = div(vi, GROUP)
    g = mod(vi, GROUP)
    ylo = div(g, 2)
    core = mod(g, 2)
    x = div(bi, 2)
    yhi = mod(bi, 2)
    y = yhi * 2 + ylo
    odd_x = mod(x, 2)
    base = z * GROUP
    g_core = ylo * 2 + 1 - core
    g_y = (1 - ylo) * 2 + core
    g_diag = (1 - ylo) * 2 + 1 - core
    core_dev = (base + g_core, bi)
    band_next = x * 2 + div(mod(y + 1, 4), 2)
    band_prev = x * 2 + div(mod(y + 3, 4), 2)
    band_far = x * 2 + 1 - yhi
    right = (vi, mod(x + 1, 4) * 2 + yhi)
    left = (vi, mod(x + 3, 4) * 2 + yhi)
    member = g * 2 + yhi

    def flip(bit, by):
        return mod(bit + by, 2)

    def member_dev(j):
        other = flip(ylo, j // 4) * 2 + flip(core, (j // 2) % 2)
        return (base + other, x * 2 + flip(yhi, j % 2))

    def place_off(i):
        a, b = div(i, 4), mod(i, 4)
        da = 4 - div(a + 1, 2) * mod(a, 2) + div(a, 2) * (1 - mod(a, 2))
        db = 2 - div(b + 1, 2) * mod(b, 2) + div(b, 2) * (1 - mod(b, 2))
        return mod(z + da, NZ), mod(x + db, 4)

    barrier = pltpu.get_barrier_semaphore()
    near = [member_dev(j) for j in range(1, 8)]
    near += [(vi, mod(x + j, 4) * 2 + yhi) for j in range(1, 4)]
    near += [(mod(z + j, NZ) * GROUP + g, bi) for j in (1, NZ - 1)]
    for device in near:
        pl.semaphore_signal(barrier, inc=1, device_id=device, device_id_type=MESH)

    local_copies = [
        pltpu.make_async_copy(src, dst, lsem.at[k])
        for k, (src, dst) in enumerate((
            (fields, field_v), (stem_out, wbuf.at[0]), (stem_in, sbuf.at[0]), (ids_hbm, ids),
            (table_hbm, table), (query_hbm, query), (kvw_hbm, kvw), (regions_hbm, regions),
            (outw_hbm, outw),
        ))
    ]
    for copy in local_copies:
        copy.start()

    pl.semaphore_wait(barrier, len(near))

    def piece_copy(src, s, u, j, send, target):
        at = pl.ds(*PIECES[j])
        return pltpu.make_async_remote_copy(
            src_ref=src.at[u, at, :], dst_ref=wbuf.at[s, u, at, :],
            send_sem=send, recv_sem=wr.at[s, u, j], device_id=target, device_id_type=MESH,
        )

    def whole_copy(u, send):
        return pltpu.make_async_remote_copy(
            src_ref=stem_out.at[u], dst_ref=wbuf.at[1, u], send_sem=send,
            recv_sem=wr.at[1, u, 0], device_id=core_dev, device_id_type=MESH,
        )

    def pixel_copy(k, source, target):
        return pltpu.make_async_remote_copy(
            src_ref=pown.at[source], dst_ref=pbuf.at[k + 1], send_sem=ps.at[k],
            recv_sem=pr.at[k], device_id=target, device_id_type=MESH,
        )

    def stem_copy(k, target):
        return pltpu.make_async_remote_copy(
            src_ref=stem_in, dst_ref=sbuf.at[k + 1], send_sem=ss.at[k],
            recv_sem=sr.at[k], device_id=target, device_id_type=MESH,
        )

    next_dev = (base + g_y, band_next)
    prev_dev = (base + g_y, band_prev)
    sends = [
        piece_copy(stem_out, 2, odd_x, 0, ws.at[0], next_dev),
        piece_copy(stem_out, 2, odd_x, 1, ws.at[1], prev_dev),
        whole_copy(0, ws.at[6]),
        stem_copy(0, core_dev),
        stem_copy(1, (base + g_y, band_far)),
        stem_copy(2, (base + g_diag, band_far)),
        whole_copy(1, ws.at[7]),
    ]
    later = [
        pixel_copy(0, g_core, core_dev),
        pixel_copy(1, g_y, (base + g_y, bi)),
        pixel_copy(2, g_diag, (base + g_diag, bi)),
    ]
    for copy in sends:
        copy.start()
    local_copies[0].wait()
    ff = field_v[...].astype(F32).reshape(2, NZ, GROUP, 8, 128)
    for k in range(GROUP):
        pown[k] = ff[:, :, k].reshape(2 * NZ * 8, 128).astype(BF16)
    for copy in later:
        copy.start()
    held = [
        piece_copy(stem_out, 2, odd_x, 2, ws.at[2], next_dev),
        piece_copy(stem_out, 2, odd_x, 3, ws.at[3], prev_dev),
        piece_copy(stem_out, 2, 1 - odd_x, 2, ws.at[4], next_dev),
        piece_copy(stem_out, 2, 1 - odd_x, 3, ws.at[5], prev_dev),
    ]
    sends = sends + later + held
    pbuf[0] = pown[g]

    def forward_x(j, target):
        return piece_copy(wbuf.at[2], 2, odd_x, j, xs.at[j], target)

    def forward_core(u, j):
        at = pl.ds(*PIECES[j])
        return pltpu.make_async_remote_copy(
            src_ref=wbuf.at[2, u, at, :], dst_ref=wbuf.at[3, u, at, :],
            send_sem=fs.at[u, j], recv_sem=wr.at[3, u, j], device_id=core_dev, device_id_type=MESH,
        )

    def arrived(s, u, j):
        piece_copy(stem_out, s, u, j, ws.at[0], core_dev).wait_recv()

    def take_rest(u, pieces):
        for j in pieces:
            forward_core(u, j).start()

    tile[...] = (
        (div(iota((512, 128), 0), 128) == div(iota((512, 128), 1), 4))
        & (mod(iota((512, 128), 0), 4) == mod(iota((512, 128), 1), 4))
    ).astype(F32).astype(BF16)
    for l in range(LATENT):
        lane = iota((128, 1024), 1)
        want = div(mod(lane, WIDTH), HEAD) + l * HEADS + div(lane, WIDTH) * 64
        ex[l] = (iota((128, 1024), 0) == want).astype(F32).astype(BF16)
    for copy in local_copies[3:5]:
        copy.wait()
    onehot = (iota((128, 64), 0) == ids[...]).astype(F32)
    emb[...] = dot(onehot.T.astype(BF16), table[...])
    for copy in local_copies[5:8]:
        copy.wait()
    qf = query[...].astype(F32)
    heads = iota((HEADS, WIDTH), 0) == div(iota((HEADS, WIDTH), 1), HEAD)
    qmat = jnp.concatenate(
        [jnp.where(heads, jnp.broadcast_to(qf[l:l + 1], (HEADS, WIDTH)), 0.0) for l in range(LATENT)],
        axis=0,
    ).astype(BF16)
    folded = dot_nt(qmat, kvw[:, :WIDTH]) * (LOG2E / HEAD**0.5)
    high = folded.astype(BF16).astype(F32)
    qk[...] = jnp.concatenate([high, folded - high], axis=0).T.astype(BF16)

    ones = jnp.ones((128, 128), F32)
    same_tile = div(iota((128, 128), 0), 16) == div(iota((128, 128), 1), 16)
    slot_row = iota((128, 128), 0)
    tile_lane = div(iota((128, 128), 1), 16)
    dest = iota((NVAR, 128), 0)
    dest_region = (div(dest, 4) * GROUP + g) * NBAND + mod(dest, 4) * 2 + yhi
    picked = jnp.zeros((NVAR, 128), F32)

    def slots(row):
        across = row.astype(F32) * ones
        below = jnp.where((across.T < across) & same_tile, 0.5, 0.0)
        return jnp.sum(below, axis=0, keepdims=True).astype(I32)

    for k in range(GROUP):
        row = regions[pl.ds(base + k, 1), :]
        hit = (slots(row) == mod(slot_row, 8)) & (div(slot_row, 32) == k) & (
            tile_lane == x * 2 + mod(div(slot_row, 16), 2)
        )
        in_region = (row == dest_region).astype(F32).astype(BF16)
        picked = picked + dot_nt(in_region, jnp.where(hit, 0.5, 0.0).astype(BF16))
    upper = mod(div(iota((NVAR, 128), 1), 8), 2) == 1
    chosen[...] = jnp.concatenate(
        [jnp.where(upper, 0.0, picked), jnp.where(upper, picked, 0.0)], axis=0
    ).astype(BF16)
    own_row = regions[pl.ds(vi, 1), :]
    own_hit = (slots(own_row) == iota((8, 128), 0)) & (div(iota((8, 128), 1), 16) == bi)
    cell = div(mod(iota((128, CHUNK), 1), HALF), 2)
    average = jnp.where(mod(iota((128, CHUNK), 0), 16) == cell, 0.25, 0.0).astype(BF16)
    pair_mean = dot(own_hit.astype(F32).astype(BF16), average).astype(BF16)
    region = vi * NBAND + bi
    count = jnp.sum((regions[...] == region).astype(F32))

    local_copies[1].wait()
    local_copies[2].wait()
    patch_mask = div(iota((HALF, 128), 1), 4) == iota((HALF, 128), 0)

    def which(t):
        late = div(t, 4)
        second = div(t, 6)
        return (
            (1 - late) * div(t, 2) + late * (2 + mod(t, 2)),
            (1 - late) * mod(t, 2) + late * (odd_x + second - 2 * odd_x * second),
        )

    def first_matrix(t):
        s, u = which(t)
        for k in range(3):
            @pl.when(t == (2, 4, 5)[k])
            def _():
                pixel_copy(k, 0, core_dev).wait_recv()
                stem_copy(k, core_dev).wait_recv()

        fscr[...] = pbuf[s, pl.ds(pl.multiple_of(u * CHUNK, CHUNK), CHUNK), :].astype(F32)
        for a in range(16):
            for i in range(4):
                row = jnp.broadcast_to(fscr[pl.ds(a * 4 + i, 1), :], (HALF, 128))
                lhs[pl.ds(a * HALF, HALF), pl.ds(i * 128, 128)] = jnp.where(
                    patch_mask, row, 0.0
                ).astype(BF16)
        pixels = dot(lhs[...], tile[...]).astype(BF16)[:, :16]
        h = dot(pixels, sbuf[s, u])
        stem = 0.5 * h * (1.0 + jnp.tanh(0.7978845608028654 * (h + 0.044715 * (h * h * h))))
        normed[t] = stem.astype(BF16)

    def second_matrix(t):
        s, u = which(t)

        @pl.when(t == 1)
        def _():
            for copy in held[:2]:
                copy.start()

        @pl.when(t == 2)
        def _():
            whole_copy(0, ws.at[0]).wait_recv()

        @pl.when(t == 3)
        def _():
            for j in range(2):
                arrived(2, odd_x, j)
                forward_x(j, (right, left)[j]).start()
            for copy in held[2:]:
                copy.start()
            take_rest(odd_x, range(2))
            whole_copy(1, ws.at[0]).wait_recv()

        @pl.when(t == 4)
        def _():
            for j in (2, 3):
                arrived(2, odd_x, j)
            take_rest(odd_x, (2, 3))

        @pl.when(t == 6)
        def _():
            for j in range(4):
                arrived(2, 1 - odd_x, j)
                forward_core(1 - odd_x, j).start()

        @pl.when((t == 5) | (t == 7))
        def _():
            for j in range(4):
                arrived(3, u, j)

        tokens = dot(normed[t], wbuf[s, u]).astype(BF16).astype(F32)
        src_g = mod(s, 2)
        src_core = core + src_g - 2 * core * src_g
        up = div(s, 2)
        src_y = ylo + up - 2 * ylo * up
        var = (base + src_y * 2 + src_core) * 2 + u
        keyed = tokens + emb[pl.ds(var, 1), :]
        centre = jnp.mean(keyed, axis=-1, keepdims=True)
        away = keyed - centre
        spread = jnp.mean(away * away, axis=-1, keepdims=True)
        normed[t] = (away * lax.rsqrt(spread + 1e-05)).astype(BF16)

    def one_variable(t, carry):
        @pl.when(t < 8)
        def _():
            first_matrix(t)

        @pl.when(t > 0)
        def _():
            second_matrix(t - 1)

        return carry

    lax.fori_loop(0, 9, one_variable, 0)

    low_lanes = iota((CHUNK, 128), 1) < 64

    def ring_copies(dr, d, half):
        off = mod(d + dr * (8 - 2 * d), 8)
        target = (mod(z + 1 + 6 * dr, NZ) * GROUP + g, bi)
        start = pl.multiple_of(half * HALF, HALF)
        return (
            pltpu.make_async_remote_copy(
                src_ref=ms.at[off, pl.ds(pl.multiple_of(half * 16, 16), 16), :], dst_ref=rms.at[dr, d - 1, half],
                send_sem=mss.at[dr, d - 1, half], recv_sem=msr.at[dr, d - 1, half],
                device_id=target, device_id_type=MESH,
            ),
            pltpu.make_async_remote_copy(
                src_ref=part.at[off, pl.ds(start, HALF), :], dst_ref=rpart.at[dr, d - 1, half],
                send_sem=os.at[dr, d - 1, half], recv_sem=orr.at[dr, d - 1, half],
                device_id=target, device_id_type=MESH,
            ),
        )

    def ring_send(dr, d, half):
        for copy in ring_copies(dr, d, half):
            copy.start()

    def put_level(off, half, level):
        ms[off, pl.ds(pl.multiple_of(half * 16, 16), 16), :] = jnp.where(low_lanes[:16], level[:16], level[16:])

    def both_lanes(packed):
        turned = pltpu.roll(packed, 64, 1)
        low = low_lanes[:16]
        return [jnp.where(low, packed, turned), jnp.where(low, turned, packed)]

    def local(off):
        start = pl.multiple_of(mod(z + off, NZ) * CHUNK, CHUNK)
        nb = normed[:, pl.ds(start, CHUNK), :].reshape(8 * CHUNK, WIDTH)
        scores = dot(nb, qk[...])
        scores = (scores + pltpu.roll(scores, 64, 1)).reshape(8, CHUNK, 128)
        top = jnp.max(scores, axis=0)
        level = top + jnp.log2(jnp.sum(jnp.exp2(scores - top[None]), axis=0))
        p = jnp.exp2(scores - jnp.ceil(level)[None])
        put_level(off, 0, level[:HALF])
        put_level(off, 1, level[HALF:])
        pb = p.astype(BF16).reshape(8 * CHUNK, 128)
        values = dot(nb, kvw[:, WIDTH:])
        for l in range(LATENT):
            wide = dot(pb, ex[l, :, :WIDTH])
            part[off, :, l * WIDTH:(l + 1) * WIDTH] = jnp.sum(
                (wide * values).reshape(8, CHUNK, WIDTH), axis=0
            ).astype(BF16)

    def offset(dr, d):
        return mod(d + dr * (8 - 2 * d), 8)

    def incoming(d, i):
        for dr, h in ((0, 1 - i), (1, i)):
            for copy in ring_copies(dr, d + 1, h):
                copy.wait_recv()
        parts = []
        for dr, h in ((0, 1 - i), (1, i)):
            parts.append((dr, h, offset(dr, d), pl.ds(pl.multiple_of(h * HALF, HALF), HALF)))
        mine, other = [], []
        for dr, h, off, _ in parts:
            mine += both_lanes(ms[off, pl.ds(pl.multiple_of(h * 16, 16), 16), :])
            other += both_lanes(rms[dr, d, h])
        level1 = jnp.concatenate(mine, axis=0)
        level2 = jnp.concatenate(other, axis=0)
        m1 = jnp.ceil(level1)
        m2 = jnp.ceil(level2)
        top = jnp.maximum(m1, m2)
        level = top + jnp.log2(jnp.exp2(level1 - top) + jnp.exp2(level2 - top))
        m = jnp.ceil(level)
        return parts, level, jnp.exp2(m1 - m), jnp.exp2(m2 - m)

    def merge(d, i):
        parts, level, a1, a2 = incoming(d, i)
        ab = jnp.where(low_lanes, a2, a1).astype(BF16)
        for k, (_, h, off, _) in enumerate(parts):
            put_level(off, h, level[k * HALF:(k + 1) * HALF])
        for l in range(LATENT):
            cols = slice(l * WIDTH, (l + 1) * WIDTH)
            factor = dot(ab, ex[l])
            for k, (dr, h, off, at) in enumerate(parts):
                lines = slice(k * HALF, (k + 1) * HALF)
                part[off, at, cols] = (
                    factor[lines, :WIDTH] * rpart[dr, d, h, :, cols].astype(F32)
                    + factor[lines, WIDTH:] * part[off, at, cols].astype(F32)
                ).astype(BF16)

    def one_chunk(k, carry):
        odd = mod(k, 2)
        d = 3 - div(k - 2, 2)
        i = mod(k, 2)

        @pl.when(k < 8)
        def _():
            local(4 - div(k + 1, 2) * odd + div(k, 2) * (1 - odd))

        @pl.when(k == 0)
        def _():
            ring_send(0, 4, 0)
            ring_send(1, 4, 1)

        @pl.when(k > 2)
        def _():
            merge(d, i)

        @pl.when((k > 1) & (k < 8))
        def _():
            ring_send(0, d, 1 - i)
            ring_send(1, d, i)

        return carry

    lax.fori_loop(0, 9, one_chunk, 0)

    _, level, a1, a2 = incoming(0, 1)
    weight = jnp.where(low_lanes, a2, a1) * jnp.exp2(jnp.ceil(level) - level)
    weight_high = weight.astype(BF16).astype(F32)
    ab = jnp.concatenate([weight_high, weight - weight_high], axis=0).astype(BF16)
    mixed = []
    for l in range(LATENT):
        cols = slice(l * WIDTH, (l + 1) * WIDTH)
        factor = dot(ab, ex[l])
        factor = factor[:CHUNK] + factor[CHUNK:]
        received = jnp.concatenate([rpart[0, 0, 0, :, cols], rpart[1, 0, 1, :, cols]], axis=0)
        mixed.append(
            (factor[:, :WIDTH] * received.astype(F32)
             + factor[:, WIDTH:] * part[0, :, cols].astype(F32)).astype(BF16)
        )
    local_copies[8].wait()
    projected = dot(jnp.concatenate(mixed, axis=0), outw[...])
    sums = []
    for l in range(LATENT):
        cols = slice(l * WIDTH, (l + 1) * WIDTH)
        out = (projected[l * CHUNK:(l + 1) * CHUNK] + qf[l:l + 1]).astype(BF16)
        lat[:, cols] = out
        sums.append(dot(pair_mean, out))
    pairs[member] = jnp.concatenate(
        [jnp.concatenate(sums[:2], axis=1), jnp.concatenate(sums[2:], axis=1)], axis=0
    ).astype(BF16)

    def pair_copy(j, slot):
        return pltpu.make_async_remote_copy(
            src_ref=pairs.at[slot], dst_ref=pairs.at[slot], send_sem=cs.at[j], recv_sem=cr.at[j],
            device_id=member_dev(j), device_id_type=MESH,
        )

    order = (1, 3, 5, 4, 7, 6, 2)
    for j in order:
        pair_copy(j, member).start()
    for j in order:
        other = (flip(ylo, j // 4) * 2 + flip(core, (j // 2) % 2)) * 2 + flip(yhi, j % 2)
        pair_copy(j, other).wait_recv()
    by_dest = dot(chosen[...], pairs[...].reshape(128, 2 * WIDTH))
    for k in range(16):
        table_f[:, k, :] = by_dest[(k // 8) * NVAR:(k // 8 + 1) * NVAR, (k % 8) * 128:(k % 8 + 1) * 128]
    table_b[...] = table_f[...].astype(BF16)

    def row_copy(i):
        to_z, to_x = place_off(i)
        return pltpu.make_async_remote_copy(
            src_ref=table_b.at[to_z * 4 + to_x], dst_ref=rows.at[i], send_sem=ts.at[i],
            recv_sem=tr.at[i], device_id=(to_z * GROUP + g, to_x * 2 + yhi), device_id_type=MESH,
        )

    def row_send(j, carry):
        row_copy(j).start()
        return carry

    def row_wait(j, carry):
        row_copy(j).wait_recv()
        return carry

    lax.fori_loop(0, NVAR - 1, row_send, 0)
    rows[NVAR - 1] = table_b[z * 4 + x]
    for copy in sends:
        copy.wait_send()
    for j in range(2):
        forward_x(j, (right, left)[j]).wait_send()
    for j in range(4):
        forward_core(0, j).wait_send()
        forward_core(1, j).wait_send()

    def ring_over(i, carry):
        dr = mod(i, 2)
        half = mod(div(i, 2), 2)
        d = 1 + div(i, 4)

        @pl.when((d < 4) | (half == dr))
        def _():
            for copy in ring_copies(dr, d, half):
                copy.wait_send()

        return carry

    for j in order:
        pair_copy(j, member).wait_send()

    def row_over(j, carry):
        row_copy(j).wait_send()
        return carry

    lax.fori_loop(0, 16, ring_over, 0)
    lax.fori_loop(0, NVAR - 1, row_over, 0)
    lax.fori_loop(0, NVAR - 1, row_wait, 0)
    total = jnp.sum(rows[...].astype(F32), axis=0) / count
    for l in range(LATENT):
        for k in range(4):
            means[0, l:l + 1, k * 128:(k + 1) * 128] = total[l * 4 + k:l * 4 + k + 1, :]


def shards(fields, stem_in, stem_out, level_ids, level_table, latent_query, kv_weight, out_weight, region_ids):
    vmem = pl.BlockSpec(memory_space=pltpu.VMEM)
    dma = pltpu.SemaphoreType.DMA
    lat, means = pl.pallas_call(
        kernel,
        out_shape=(
            jax.ShapeDtypeStruct((CHUNK, FLAT), BF16),
            jax.ShapeDtypeStruct((1, LATENT, WIDTH), F32),
        ),
        in_specs=[pl.BlockSpec(memory_space=pl.ANY)] * 9,
        out_specs=(vmem, vmem),
        scratch_shapes=[
            pltpu.VMEM((2, 256, 128), BF16),
            pltpu.VMEM((1, 64), I32),
            pltpu.VMEM((128, WIDTH), BF16),
            pltpu.VMEM((LATENT, WIDTH), BF16),
            pltpu.VMEM((WIDTH, 2 * WIDTH), BF16),
            pltpu.VMEM((WIDTH, WIDTH), BF16),
            pltpu.VMEM((32, 128), I32),
            pltpu.VMEM((GROUP, 128, 128), BF16),
            pltpu.VMEM((GROUP, 128, 128), BF16),
            pltpu.VMEM((GROUP, 2, 16, WIDTH), BF16),
            pltpu.VMEM((GROUP, 2, WIDTH, WIDTH), BF16),
            pltpu.VMEM((CHUNK, 128), F32),
            pltpu.VMEM((512, 512), BF16),
            pltpu.VMEM((512, 128), BF16),
            pltpu.VMEM((8, 512, WIDTH), BF16),
            pltpu.VMEM((64, WIDTH), F32),
            pltpu.VMEM((WIDTH, 128), BF16),
            pltpu.VMEM((LATENT, 128, 2 * WIDTH), BF16),
            pltpu.VMEM((NZ, CHUNK, FLAT), BF16),
            pltpu.VMEM((NZ, HALF, 128), F32),
            pltpu.VMEM((2, 4, 2, HALF, FLAT), BF16),
            pltpu.VMEM((2, 4, 2, 16, 128), F32),
            pltpu.VMEM((2 * NVAR, 128), BF16),
            pltpu.VMEM((8, 16, 2 * WIDTH), BF16),
            pltpu.VMEM((NVAR, 16, 128), F32),
            pltpu.VMEM((NVAR, 16, 128), BF16),
            pltpu.VMEM((NVAR, 16, 128), BF16),
            dma((9,)),
            dma((3,)), dma((3,)),
            dma((3,)), dma((3,)),
            dma((8,)), dma((GROUP, 2, 4)), dma((2,)), dma((2, 4)),
            dma((2, 4, 2)), dma((2, 4, 2)),
            dma((2, 4, 2)), dma((2, 4, 2)),
            dma((8,)), dma((8,)),
            dma((NVAR,)), dma((NVAR,)),
        ],
        compiler_params=pltpu.CompilerParams(
            collective_id=0, has_side_effects=True, vmem_limit_bytes=60 * 1024 * 1024
        ),
        name="window",
    )(
        fields, stem_in, stem_out, level_ids.reshape(1, -1), level_table, latent_query,
        kv_weight, out_weight, region_ids,
    )
    return lat.reshape(2, 32, LATENT, WIDTH), means


def solution(mesh):
    in_specs = (
        P("var", None, "band"),
        P("var", None, None),
        P("var", None, None),
        P(),
        P(),
        P(),
        P(),
        P(),
        P(),
    )
    out_specs = (P("var", "band", None, None), P(("var", "band"), None, None))
    return jax.shard_map(shards, mesh=mesh, in_specs=in_specs, out_specs=out_specs, check_vma=False)
```

```python
import jax
import jax.numpy as jnp
from jax import lax
from jax.experimental import pallas as pl
from jax.experimental.pallas import tpu as pltpu
from jax.sharding import PartitionSpec as P

MESH = pl.DeviceIdType.MESH
BF16 = jnp.bfloat16
F32 = jnp.float32
I32 = jnp.int32

HEADS = 16
HEAD = 32
WIDTH = 512
LATENT = 4
FLAT = LATENT * WIDTH
NZ = 8
GROUP = 4
NVAR = 32
NBAND = 8
CHUNK = 64
HALF = 32
LOG2E = 1.4426950408889634
PIECES = ((0, 128), (128, 128), (256, 128), (384, 128))


def iota(shape, axis):
    return lax.broadcasted_iota(I32, shape, axis)


def dot(a, b):
    return jnp.dot(a, b, preferred_element_type=F32)


def dot_nt(a, b):
    return lax.dot_general(a, b, (((1,), (1,)), ((), ())), preferred_element_type=F32)


def mod(a, n):
    return lax.rem(a, jnp.int32(n))


def div(a, n):
    return lax.div(a, jnp.int32(n))


def kernel(
    fields, stem_in, stem_out, ids_hbm, table_hbm, query, kvw_hbm, outw_hbm, regions_hbm,
    lat, means,
    field_v, ids, table, kvw, outw, regions,
    pbuf, pown, sbuf, wbuf, fscr, lhs, tile, normed, emb, qk, ex,
    part, ms, rpart, rms, chosen, pairs, table_f, table_b, rows,
    lsem, ps, pr, ss, sr, ws, wr, xs, fs, os, orr, mss, msr, cs, cr, ts, tr,
):
    vi = lax.axis_index("var")
    bi = lax.axis_index("band")
    z = div(vi, GROUP)
    g = mod(vi, GROUP)
    ylo = div(g, 2)
    core = mod(g, 2)
    x = div(bi, 2)
    yhi = mod(bi, 2)
    y = yhi * 2 + ylo
    odd_x = mod(x, 2)
    base = z * GROUP
    g_core = ylo * 2 + 1 - core
    g_y = (1 - ylo) * 2 + core
    g_diag = (1 - ylo) * 2 + 1 - core
    core_dev = (base + g_core, bi)
    band_next = x * 2 + div(mod(y + 1, 4), 2)
    band_prev = x * 2 + div(mod(y + 3, 4), 2)
    band_far = x * 2 + 1 - yhi
    right = (vi, mod(x + 1, 4) * 2 + yhi)
    left = (vi, mod(x + 3, 4) * 2 + yhi)
    member = g * 2 + yhi

    def flip(bit, by):
        return mod(bit + by, 2)

    def member_dev(j):
        other = flip(ylo, j // 4) * 2 + flip(core, (j // 2) % 2)
        return (base + other, x * 2 + flip(yhi, j % 2))

    def place_off(i):
        a, b = div(i, 4), mod(i, 4)
        da = 4 - div(a + 1, 2) * mod(a, 2) + div(a, 2) * (1 - mod(a, 2))
        db = 2 - div(b + 1, 2) * mod(b, 2) + div(b, 2) * (1 - mod(b, 2))
        return mod(z + da, NZ), mod(x + db, 4)

    barrier = pltpu.get_barrier_semaphore()
    near = [member_dev(j) for j in range(1, 8)]
    near += [(vi, mod(x + j, 4) * 2 + yhi) for j in range(1, 4)]
    near += [(mod(z + j, NZ) * GROUP + g, bi) for j in (1, NZ - 1)]
    for device in near:
        pl.semaphore_signal(barrier, inc=1, device_id=device, device_id_type=MESH)

    local_copies = [
        pltpu.make_async_copy(src, dst, lsem.at[k])
        for k, (src, dst) in enumerate((
            (fields, field_v), (stem_out, wbuf.at[0]), (stem_in, sbuf.at[0]), (ids_hbm, ids),
            (table_hbm, table), (kvw_hbm, kvw), (regions_hbm, regions),
            (outw_hbm, outw),
        ))
    ]
    for copy in local_copies:
        copy.start()

    pl.semaphore_wait(barrier, len(near))

    def piece_copy(src, s, u, j, send, target):
        at = pl.ds(*PIECES[j])
        return pltpu.make_async_remote_copy(
            src_ref=src.at[u, at, :], dst_ref=wbuf.at[s, u, at, :],
            send_sem=send, recv_sem=wr.at[s, u, j], device_id=target, device_id_type=MESH,
        )

    def whole_copy(u, send):
        return pltpu.make_async_remote_copy(
            src_ref=stem_out.at[u], dst_ref=wbuf.at[1, u], send_sem=send,
            recv_sem=wr.at[1, u, 0], device_id=core_dev, device_id_type=MESH,
        )

    def pixel_copy(k, source, target):
        return pltpu.make_async_remote_copy(
            src_ref=pown.at[source], dst_ref=pbuf.at[k + 1], send_sem=ps.at[k],
            recv_sem=pr.at[k], device_id=target, device_id_type=MESH,
        )

    def stem_copy(k, target):
        return pltpu.make_async_remote_copy(
            src_ref=stem_in, dst_ref=sbuf.at[k + 1], send_sem=ss.at[k],
            recv_sem=sr.at[k], device_id=target, device_id_type=MESH,
        )

    next_dev = (base + g_y, band_next)
    prev_dev = (base + g_y, band_prev)
    sends = [
        piece_copy(stem_out, 2, odd_x, 0, ws.at[0], next_dev),
        piece_copy(stem_out, 2, odd_x, 1, ws.at[1], prev_dev),
        whole_copy(0, ws.at[6]),
        stem_copy(0, core_dev),
        stem_copy(1, (base + g_y, band_far)),
        stem_copy(2, (base + g_diag, band_far)),
        whole_copy(1, ws.at[7]),
    ]
    later = [
        pixel_copy(0, g_core, core_dev),
        pixel_copy(1, g_y, (base + g_y, bi)),
        pixel_copy(2, g_diag, (base + g_diag, bi)),
    ]
    for copy in sends:
        copy.start()
    local_copies[0].wait()
    ff = field_v[...].astype(F32).reshape(2, NZ, GROUP, 8, 128)
    for k in range(GROUP):
        pown[k] = ff[:, :, k].reshape(2 * NZ * 8, 128).astype(BF16)
    for copy in later:
        copy.start()
    held = [
        piece_copy(stem_out, 2, odd_x, 2, ws.at[2], next_dev),
        piece_copy(stem_out, 2, odd_x, 3, ws.at[3], prev_dev),
        piece_copy(stem_out, 2, 1 - odd_x, 2, ws.at[4], next_dev),
        piece_copy(stem_out, 2, 1 - odd_x, 3, ws.at[5], prev_dev),
    ]
    sends = sends + later + held
    pbuf[0] = pown[g]

    def forward_x(j, target):
        return piece_copy(wbuf.at[2], 2, odd_x, j, xs.at[j], target)

    def forward_core(u, j):
        at = pl.ds(*PIECES[j])
        return pltpu.make_async_remote_copy(
            src_ref=wbuf.at[2, u, at, :], dst_ref=wbuf.at[3, u, at, :],
            send_sem=fs.at[u, j], recv_sem=wr.at[3, u, j], device_id=core_dev, device_id_type=MESH,
        )

    def arrived(s, u, j):
        piece_copy(stem_out, s, u, j, ws.at[0], core_dev).wait_recv()

    def take_rest(u, pieces):
        for j in pieces:
            forward_core(u, j).start()

    tile[...] = (
        (div(iota((512, 128), 0), 128) == div(iota((512, 128), 1), 4))
        & (mod(iota((512, 128), 0), 4) == mod(iota((512, 128), 1), 4))
    ).astype(F32).astype(BF16)
    for l in range(LATENT):
        lane = iota((128, 1024), 1)
        want = div(mod(lane, WIDTH), HEAD) + l * HEADS + div(lane, WIDTH) * 64
        ex[l] = (iota((128, 1024), 0) == want).astype(F32).astype(BF16)
    for copy in local_copies[3:5]:
        copy.wait()
    onehot = (iota((128, 64), 0) == ids[...]).astype(F32)
    emb[...] = dot(onehot.T.astype(BF16), table[...])
    for copy in local_copies[5:7]:
        copy.wait()
    qf = query[...].astype(F32)
    heads = iota((HEADS, WIDTH), 0) == div(iota((HEADS, WIDTH), 1), HEAD)
    qmat = jnp.concatenate(
        [jnp.where(heads, jnp.broadcast_to(qf[l:l + 1], (HEADS, WIDTH)), 0.0) for l in range(LATENT)],
        axis=0,
    ).astype(BF16)
    folded = dot_nt(qmat, kvw[:, :WIDTH]) * (LOG2E / HEAD**0.5)
    high = folded.astype(BF16).astype(F32)
    qk[...] = jnp.concatenate([high, folded - high], axis=0).T.astype(BF16)

    ones = jnp.ones((128, 128), F32)
    same_tile = div(iota((128, 128), 0), 16) == div(iota((128, 128), 1), 16)
    slot_row = iota((128, 128), 0)
    tile_lane = div(iota((128, 128), 1), 16)
    dest = iota((NVAR, 128), 0)
    dest_region = (div(dest, 4) * GROUP + g) * NBAND + mod(dest, 4) * 2 + yhi
    picked = jnp.zeros((NVAR, 128), F32)

    def slots(row):
        across = row.astype(F32) * ones
        below = jnp.where((across.T < across) & same_tile, 0.5, 0.0)
        return jnp.sum(below, axis=0, keepdims=True).astype(I32)

    for k in range(GROUP):
        row = regions[pl.ds(base + k, 1), :]
        hit = (slots(row) == mod(slot_row, 8)) & (div(slot_row, 32) == k) & (
            tile_lane == x * 2 + mod(div(slot_row, 16), 2)
        )
        in_region = (row == dest_region).astype(F32).astype(BF16)
        picked = picked + dot_nt(in_region, jnp.where(hit, 0.5, 0.0).astype(BF16))
    upper = mod(div(iota((NVAR, 128), 1), 8), 2) == 1
    chosen[...] = jnp.concatenate(
        [jnp.where(upper, 0.0, picked), jnp.where(upper, picked, 0.0)], axis=0
    ).astype(BF16)
    own_row = regions[pl.ds(vi, 1), :]
    own_hit = (slots(own_row) == iota((8, 128), 0)) & (div(iota((8, 128), 1), 16) == bi)
    cell = div(mod(iota((128, CHUNK), 1), HALF), 2)
    average = jnp.where(mod(iota((128, CHUNK), 0), 16) == cell, 0.25, 0.0).astype(BF16)
    pair_mean = dot(own_hit.astype(F32).astype(BF16), average).astype(BF16)
    region = vi * NBAND + bi
    count = jnp.sum((regions[...] == region).astype(F32))

    local_copies[1].wait()
    local_copies[2].wait()
    patch_mask = div(iota((HALF, 128), 1), 4) == iota((HALF, 128), 0)

    def which(t):
        late = div(t, 4)
        second = div(t, 6)
        return (
            (1 - late) * div(t, 2) + late * (2 + mod(t, 2)),
            (1 - late) * mod(t, 2) + late * (odd_x + second - 2 * odd_x * second),
        )

    def first_matrix(t):
        s, u = which(t)
        for k in range(3):
            @pl.when(t == (2, 4, 5)[k])
            def _():
                pixel_copy(k, 0, core_dev).wait_recv()
                stem_copy(k, core_dev).wait_recv()

        fscr[...] = pbuf[s, pl.ds(pl.multiple_of(u * CHUNK, CHUNK), CHUNK), :].astype(F32)
        for a in range(16):
            for i in range(4):
                row = jnp.broadcast_to(fscr[pl.ds(a * 4 + i, 1), :], (HALF, 128))
                lhs[pl.ds(a * HALF, HALF), pl.ds(i * 128, 128)] = jnp.where(
                    patch_mask, row, 0.0
                ).astype(BF16)
        pixels = dot(lhs[...], tile[...]).astype(BF16)[:, :16]
        h = dot(pixels, sbuf[s, u])
        stem = 0.5 * h * (1.0 + jnp.tanh(0.7978845608028654 * (h + 0.044715 * (h * h * h))))
        normed[t] = stem.astype(BF16)

    def second_matrix(t):
        s, u = which(t)

        @pl.when(t == 1)
        def _():
            for copy in held[:2]:
                copy.start()

        @pl.when(t == 2)
        def _():
            whole_copy(0, ws.at[0]).wait_recv()

        @pl.when(t == 3)
        def _():
            for j in range(2):
                arrived(2, odd_x, j)
                forward_x(j, (right, left)[j]).start()
            for copy in held[2:]:
                copy.start()
            take_rest(odd_x, range(2))
            whole_copy(1, ws.at[0]).wait_recv()

        @pl.when(t == 4)
        def _():
            for j in (2, 3):
                arrived(2, odd_x, j)
            take_rest(odd_x, (2, 3))

        @pl.when(t == 6)
        def _():
            for j in range(4):
                arrived(2, 1 - odd_x, j)
                forward_core(1 - odd_x, j).start()

        @pl.when((t == 5) | (t == 7))
        def _():
            for j in range(4):
                arrived(3, u, j)

        tokens = dot(normed[t], wbuf[s, u]).astype(BF16).astype(F32)
        src_g = mod(s, 2)
        src_core = core + src_g - 2 * core * src_g
        up = div(s, 2)
        src_y = ylo + up - 2 * ylo * up
        var = (base + src_y * 2 + src_core) * 2 + u
        keyed = tokens + emb[pl.ds(var, 1), :]
        centre = jnp.mean(keyed, axis=-1, keepdims=True)
        away = keyed - centre
        spread = jnp.mean(away * away, axis=-1, keepdims=True)
        normed[t] = (away * lax.rsqrt(spread + 1e-05)).astype(BF16)

    def one_variable(t, carry):
        @pl.when(t < 8)
        def _():
            first_matrix(t)

        @pl.when(t > 0)
        def _():
            second_matrix(t - 1)

        return carry

    lax.fori_loop(0, 9, one_variable, 0)

    low_lanes = iota((CHUNK, 128), 1) < 64

    def ring_copies(dr, d, half):
        off = mod(d + dr * (8 - 2 * d), 8)
        target = (mod(z + 1 + 6 * dr, NZ) * GROUP + g, bi)
        start = pl.multiple_of(half * HALF, HALF)
        return (
            pltpu.make_async_remote_copy(
                src_ref=ms.at[off, pl.ds(pl.multiple_of(half * 16, 16), 16), :], dst_ref=rms.at[dr, d - 1, half],
                send_sem=mss.at[dr, d - 1, half], recv_sem=msr.at[dr, d - 1, half],
                device_id=target, device_id_type=MESH,
            ),
            pltpu.make_async_remote_copy(
                src_ref=part.at[off, pl.ds(start, HALF), :], dst_ref=rpart.at[dr, d - 1, half],
                send_sem=os.at[dr, d - 1, half], recv_sem=orr.at[dr, d - 1, half],
                device_id=target, device_id_type=MESH,
            ),
        )

    def ring_send(dr, d, half):
        for copy in ring_copies(dr, d, half):
            copy.start()

    def put_level(off, half, level):
        ms[off, pl.ds(pl.multiple_of(half * 16, 16), 16), :] = jnp.where(low_lanes[:16], level[:16], level[16:])

    def both_lanes(packed):
        turned = pltpu.roll(packed, 64, 1)
        low = low_lanes[:16]
        return [jnp.where(low, packed, turned), jnp.where(low, turned, packed)]

    def local(off):
        start = pl.multiple_of(mod(z + off, NZ) * CHUNK, CHUNK)
        nb = normed[:, pl.ds(start, CHUNK), :].reshape(8 * CHUNK, WIDTH)
        scores = dot(nb, qk[...])
        scores = (scores + pltpu.roll(scores, 64, 1)).reshape(8, CHUNK, 128)
        top = jnp.max(scores, axis=0)
        level = top + jnp.log2(jnp.sum(jnp.exp2(scores - top[None]), axis=0))
        p = jnp.exp2(scores - jnp.ceil(level)[None])
        put_level(off, 0, level[:HALF])
        put_level(off, 1, level[HALF:])
        pb = p.astype(BF16).reshape(8 * CHUNK, 128)
        values = dot(nb, kvw[:, WIDTH:])
        for l in range(LATENT):
            wide = dot(pb, ex[l, :, :WIDTH])
            part[off, :, l * WIDTH:(l + 1) * WIDTH] = jnp.sum(
                (wide * values).reshape(8, CHUNK, WIDTH), axis=0
            ).astype(BF16)

    def offset(dr, d):
        return mod(d + dr * (8 - 2 * d), 8)

    def incoming(d, i):
        for dr, h in ((0, 1 - i), (1, i)):
            for copy in ring_copies(dr, d + 1, h):
                copy.wait_recv()
        parts = []
        for dr, h in ((0, 1 - i), (1, i)):
            parts.append((dr, h, offset(dr, d), pl.ds(pl.multiple_of(h * HALF, HALF), HALF)))
        mine, other = [], []
        for dr, h, off, _ in parts:
            mine += both_lanes(ms[off, pl.ds(pl.multiple_of(h * 16, 16), 16), :])
            other += both_lanes(rms[dr, d, h])
        level1 = jnp.concatenate(mine, axis=0)
        level2 = jnp.concatenate(other, axis=0)
        m1 = jnp.ceil(level1)
        m2 = jnp.ceil(level2)
        top = jnp.maximum(m1, m2)
        level = top + jnp.log2(jnp.exp2(level1 - top) + jnp.exp2(level2 - top))
        m = jnp.ceil(level)
        return parts, level, jnp.exp2(m1 - m), jnp.exp2(m2 - m)

    def merge(d, i):
        parts, level, a1, a2 = incoming(d, i)
        ab = jnp.where(low_lanes, a2, a1).astype(BF16)
        for k, (_, h, off, _) in enumerate(parts):
            put_level(off, h, level[k * HALF:(k + 1) * HALF])
        for l in range(LATENT):
            cols = slice(l * WIDTH, (l + 1) * WIDTH)
            factor = dot(ab, ex[l])
            for k, (dr, h, off, at) in enumerate(parts):
                lines = slice(k * HALF, (k + 1) * HALF)
                part[off, at, cols] = (
                    factor[lines, :WIDTH] * rpart[dr, d, h, :, cols].astype(F32)
                    + factor[lines, WIDTH:] * part[off, at, cols].astype(F32)
                ).astype(BF16)

    def one_chunk(k, carry):
        odd = mod(k, 2)
        d = 3 - div(k - 2, 2)
        i = mod(k, 2)

        @pl.when(k < 8)
        def _():
            local(4 - div(k + 1, 2) * odd + div(k, 2) * (1 - odd))

        @pl.when(k == 0)
        def _():
            ring_send(0, 4, 0)
            ring_send(1, 4, 1)

        @pl.when(k > 2)
        def _():
            merge(d, i)

        @pl.when((k > 1) & (k < 8))
        def _():
            ring_send(0, d, 1 - i)
            ring_send(1, d, i)

        return carry

    lax.fori_loop(0, 9, one_chunk, 0)

    _, level, a1, a2 = incoming(0, 1)
    weight = jnp.where(low_lanes, a2, a1) * jnp.exp2(jnp.ceil(level) - level)
    weight_high = weight.astype(BF16).astype(F32)
    ab = jnp.concatenate([weight_high, weight - weight_high], axis=0).astype(BF16)
    mixed = []
    for l in range(LATENT):
        cols = slice(l * WIDTH, (l + 1) * WIDTH)
        factor = dot(ab, ex[l])
        factor = factor[:CHUNK] + factor[CHUNK:]
        received = jnp.concatenate([rpart[0, 0, 0, :, cols], rpart[1, 0, 1, :, cols]], axis=0)
        mixed.append(
            (factor[:, :WIDTH] * received.astype(F32)
             + factor[:, WIDTH:] * part[0, :, cols].astype(F32)).astype(BF16)
        )
    local_copies[7].wait()
    projected = dot(jnp.concatenate(mixed, axis=0), outw[...])
    sums = []
    for l in range(LATENT):
        cols = slice(l * WIDTH, (l + 1) * WIDTH)
        out = (projected[l * CHUNK:(l + 1) * CHUNK] + qf[l:l + 1]).astype(BF16)
        lat[:, cols] = out
        sums.append(dot(pair_mean, out))
    pairs[member] = jnp.concatenate(
        [jnp.concatenate(sums[:2], axis=1), jnp.concatenate(sums[2:], axis=1)], axis=0
    ).astype(BF16)

    def pair_copy(j, slot):
        return pltpu.make_async_remote_copy(
            src_ref=pairs.at[slot], dst_ref=pairs.at[slot], send_sem=cs.at[j], recv_sem=cr.at[j],
            device_id=member_dev(j), device_id_type=MESH,
        )

    order = (1, 3, 5, 4, 7, 6, 2)
    for j in order:
        pair_copy(j, member).start()
    for j in order:
        other = (flip(ylo, j // 4) * 2 + flip(core, (j // 2) % 2)) * 2 + flip(yhi, j % 2)
        pair_copy(j, other).wait_recv()
    by_dest = dot(chosen[...], pairs[...].reshape(128, 2 * WIDTH))
    for k in range(16):
        table_f[:, k, :] = by_dest[(k // 8) * NVAR:(k // 8 + 1) * NVAR, (k % 8) * 128:(k % 8 + 1) * 128]
    table_b[...] = table_f[...].astype(BF16)

    def row_copy(i):
        to_z, to_x = place_off(i)
        return pltpu.make_async_remote_copy(
            src_ref=table_b.at[to_z * 4 + to_x], dst_ref=rows.at[i], send_sem=ts.at[i],
            recv_sem=tr.at[i], device_id=(to_z * GROUP + g, to_x * 2 + yhi), device_id_type=MESH,
        )

    def row_send(j, carry):
        row_copy(j).start()
        return carry

    def row_wait(j, carry):
        row_copy(j).wait_recv()
        return carry

    lax.fori_loop(0, NVAR - 1, row_send, 0)
    rows[NVAR - 1] = table_b[z * 4 + x]
    for copy in sends:
        copy.wait_send()
    for j in range(2):
        forward_x(j, (right, left)[j]).wait_send()
    for j in range(4):
        forward_core(0, j).wait_send()
        forward_core(1, j).wait_send()

    def ring_over(i, carry):
        dr = mod(i, 2)
        half = mod(div(i, 2), 2)
        d = 1 + div(i, 4)

        @pl.when((d < 4) | (half == dr))
        def _():
            for copy in ring_copies(dr, d, half):
                copy.wait_send()

        return carry

    for j in order:
        pair_copy(j, member).wait_send()

    def row_over(j, carry):
        row_copy(j).wait_send()
        return carry

    lax.fori_loop(0, 16, ring_over, 0)
    lax.fori_loop(0, NVAR - 1, row_over, 0)
    lax.fori_loop(0, NVAR - 1, row_wait, 0)
    total = jnp.sum(rows[...].astype(F32), axis=0) / count
    for l in range(LATENT):
        for k in range(4):
            means[0, l:l + 1, k * 128:(k + 1) * 128] = total[l * 4 + k:l * 4 + k + 1, :]


def shards(fields, stem_in, stem_out, level_ids, level_table, latent_query, kv_weight, out_weight, region_ids):
    vmem = pl.BlockSpec(memory_space=pltpu.VMEM)
    dma = pltpu.SemaphoreType.DMA
    lat, means = pl.pallas_call(
        kernel,
        out_shape=(
            jax.ShapeDtypeStruct((CHUNK, FLAT), BF16),
            jax.ShapeDtypeStruct((1, LATENT, WIDTH), F32),
        ),
        in_specs=[vmem if k == 5 else pl.BlockSpec(memory_space=pl.ANY) for k in range(9)],
        out_specs=(vmem, vmem),
        scratch_shapes=[
            pltpu.VMEM((2, 256, 128), BF16),
            pltpu.VMEM((1, 64), I32),
            pltpu.VMEM((128, WIDTH), BF16),
            pltpu.VMEM((WIDTH, 2 * WIDTH), BF16),
            pltpu.VMEM((WIDTH, WIDTH), BF16),
            pltpu.VMEM((32, 128), I32),
            pltpu.VMEM((GROUP, 128, 128), BF16),
            pltpu.VMEM((GROUP, 128, 128), BF16),
            pltpu.VMEM((GROUP, 2, 16, WIDTH), BF16),
            pltpu.VMEM((GROUP, 2, WIDTH, WIDTH), BF16),
            pltpu.VMEM((CHUNK, 128), F32),
            pltpu.VMEM((512, 512), BF16),
            pltpu.VMEM((512, 128), BF16),
            pltpu.VMEM((8, 512, WIDTH), BF16),
            pltpu.VMEM((64, WIDTH), F32),
            pltpu.VMEM((WIDTH, 128), BF16),
            pltpu.VMEM((LATENT, 128, 2 * WIDTH), BF16),
            pltpu.VMEM((NZ, CHUNK, FLAT), BF16),
            pltpu.VMEM((NZ, HALF, 128), F32),
            pltpu.VMEM((2, 4, 2, HALF, FLAT), BF16),
            pltpu.VMEM((2, 4, 2, 16, 128), F32),
            pltpu.VMEM((2 * NVAR, 128), BF16),
            pltpu.VMEM((8, 16, 2 * WIDTH), BF16),
            pltpu.VMEM((NVAR, 16, 128), F32),
            pltpu.VMEM((NVAR, 16, 128), BF16),
            pltpu.VMEM((NVAR, 16, 128), BF16),
            dma((8,)),
            dma((3,)), dma((3,)),
            dma((3,)), dma((3,)),
            dma((8,)), dma((GROUP, 2, 4)), dma((2,)), dma((2, 4)),
            dma((2, 4, 2)), dma((2, 4, 2)),
            dma((2, 4, 2)), dma((2, 4, 2)),
            dma((8,)), dma((8,)),
            dma((NVAR,)), dma((NVAR,)),
        ],
        compiler_params=pltpu.CompilerParams(
            collective_id=0, has_side_effects=True, vmem_limit_bytes=60 * 1024 * 1024
        ),
        name="window",
    )(
        fields, stem_in, stem_out, level_ids.reshape(1, -1), level_table, latent_query,
        kv_weight, out_weight, region_ids,
    )
    return lat.reshape(2, 32, LATENT, WIDTH), means


def solution(mesh):
    in_specs = (
        P("var", None, "band"),
        P("var", None, None),
        P("var", None, None),
        P(),
        P(),
        P(),
        P(),
        P(),
        P(),
    )
    out_specs = (P("var", "band", None, None), P(("var", "band"), None, None))
    return jax.shard_map(shards, mesh=mesh, in_specs=in_specs, out_specs=out_specs, check_vma=False)
```

```python
import jax
import jax.numpy as jnp
from jax import lax
from jax.experimental import pallas as pl
from jax.experimental.pallas import tpu as pltpu
from jax.sharding import PartitionSpec as P

MESH = pl.DeviceIdType.MESH
BF16 = jnp.bfloat16
F32 = jnp.float32
I32 = jnp.int32

HEADS = 16
HEAD = 32
WIDTH = 512
LATENT = 4
FLAT = LATENT * WIDTH
NZ = 8
GROUP = 4
NVAR = 32
NBAND = 8
CHUNK = 64
HALF = 32
LOG2E = 1.4426950408889634
PIECES = ((0, 128), (128, 128), (256, 128), (384, 128))


def iota(shape, axis):
    return lax.broadcasted_iota(I32, shape, axis)


def dot(a, b):
    return jnp.dot(a, b, preferred_element_type=F32)


def dot_nt(a, b):
    return lax.dot_general(a, b, (((1,), (1,)), ((), ())), preferred_element_type=F32)


def mod(a, n):
    return lax.rem(a, jnp.int32(n))


def div(a, n):
    return lax.div(a, jnp.int32(n))


def kernel(
    fields, stem_in, stem_out, ids_hbm, table_hbm, query_hbm, kvw_hbm, outw_hbm, regions_hbm,
    lat, means,
    field_v, ids, table, query, kvw, outw, regions,
    pbuf, pown, sbuf, wbuf, fscr, lhs, tile, normed, emb, qk, ex,
    part, ms, rpart, rms, chosen, pairs, table_f, table_b, rows,
    lsem, ps, pr, ss, sr, ws, wr, xs, fs, os, orr, mss, msr, cs, cr, ts, tr,
):
    vi = lax.axis_index("var")
    bi = lax.axis_index("band")
    z = div(vi, GROUP)
    g = mod(vi, GROUP)
    ylo = div(g, 2)
    core = mod(g, 2)
    x = div(bi, 2)
    yhi = mod(bi, 2)
    y = yhi * 2 + ylo
    odd_x = mod(x, 2)
    base = z * GROUP
    g_core = ylo * 2 + 1 - core
    g_y = (1 - ylo) * 2 + core
    g_diag = (1 - ylo) * 2 + 1 - core
    core_dev = (base + g_core, bi)
    band_next = x * 2 + div(mod(y + 1, 4), 2)
    band_prev = x * 2 + div(mod(y + 3, 4), 2)
    band_far = x * 2 + 1 - yhi
    right = (vi, mod(x + 1, 4) * 2 + yhi)
    left = (vi, mod(x + 3, 4) * 2 + yhi)
    member = g * 2 + yhi

    def flip(bit, by):
        return mod(bit + by, 2)

    def member_dev(j):
        other = flip(ylo, j // 4) * 2 + flip(core, (j // 2) % 2)
        return (base + other, x * 2 + flip(yhi, j % 2))

    def place_off(i):
        a, b = div(i, 4), mod(i, 4)
        da = 4 - div(a + 1, 2) * mod(a, 2) + div(a, 2) * (1 - mod(a, 2))
        db = 2 - div(b + 1, 2) * mod(b, 2) + div(b, 2) * (1 - mod(b, 2))
        return mod(z + da, NZ), mod(x + db, 4)

    barrier = pltpu.get_barrier_semaphore()
    near = [member_dev(j) for j in range(1, 8)]
    near += [(vi, mod(x + j, 4) * 2 + yhi) for j in range(1, 4)]
    near += [(mod(z + j, NZ) * GROUP + g, bi) for j in (1, NZ - 1)]
    for device in near:
        pl.semaphore_signal(barrier, inc=1, device_id=device, device_id_type=MESH)

    local_copies = [
        pltpu.make_async_copy(src, dst, lsem.at[k])
        for k, (src, dst) in enumerate((
            (fields, field_v), (stem_out, wbuf.at[0]), (stem_in, sbuf.at[0]), (ids_hbm, ids),
            (table_hbm, table), (query_hbm, query), (kvw_hbm, kvw), (regions_hbm, regions),
            (outw_hbm, outw),
        ))
    ]
    for copy in local_copies:
        copy.start()

    pl.semaphore_wait(barrier, len(near))

    def piece_copy(src, s, u, j, send, target):
        at = pl.ds(*PIECES[j])
        return pltpu.make_async_remote_copy(
            src_ref=src.at[u, at, :], dst_ref=wbuf.at[s, u, at, :],
            send_sem=send, recv_sem=wr.at[s, u, j], device_id=target, device_id_type=MESH,
        )

    def whole_copy(u, send):
        return pltpu.make_async_remote_copy(
            src_ref=stem_out.at[u], dst_ref=wbuf.at[1, u], send_sem=send,
            recv_sem=wr.at[1, u, 0], device_id=core_dev, device_id_type=MESH,
        )

    def pixel_copy(k, source, target):
        return pltpu.make_async_remote_copy(
            src_ref=pown.at[source], dst_ref=pbuf.at[k + 1], send_sem=ps.at[k],
            recv_sem=pr.at[k], device_id=target, device_id_type=MESH,
        )

    def stem_copy(k, target):
        return pltpu.make_async_remote_copy(
            src_ref=stem_in, dst_ref=sbuf.at[k + 1], send_sem=ss.at[k],
            recv_sem=sr.at[k], device_id=target, device_id_type=MESH,
        )

    next_dev = (base + g_y, band_next)
    prev_dev = (base + g_y, band_prev)
    sends = [
        piece_copy(stem_out, 2, odd_x, 0, ws.at[0], next_dev),
        piece_copy(stem_out, 2, odd_x, 1, ws.at[1], prev_dev),
        whole_copy(0, ws.at[6]),
        stem_copy(0, core_dev),
        stem_copy(1, (base + g_y, band_far)),
        stem_copy(2, (base + g_diag, band_far)),
        whole_copy(1, ws.at[7]),
    ]
    later = [
        pixel_copy(0, g_core, core_dev),
        pixel_copy(1, g_y, (base + g_y, bi)),
        pixel_copy(2, g_diag, (base + g_diag, bi)),
    ]
    for copy in sends:
        copy.start()
    local_copies[0].wait()
    ff = field_v[...].astype(F32).reshape(2, NZ, GROUP, 8, 128)
    for k in range(GROUP):
        pown[k] = ff[:, :, k].reshape(2 * NZ * 8, 128).astype(BF16)
    for copy in later:
        copy.start()
    held = [
        piece_copy(stem_out, 2, odd_x, 2, ws.at[2], next_dev),
        piece_copy(stem_out, 2, odd_x, 3, ws.at[3], prev_dev),
        piece_copy(stem_out, 2, 1 - odd_x, 2, ws.at[4], next_dev),
        piece_copy(stem_out, 2, 1 - odd_x, 3, ws.at[5], prev_dev),
    ]
    sends = sends + later + held
    pbuf[0] = pown[g]

    def forward_x(j, target):
        return piece_copy(wbuf.at[2], 2, odd_x, j, xs.at[j], target)

    def forward_core(u, j):
        at = pl.ds(*PIECES[j])
        return pltpu.make_async_remote_copy(
            src_ref=wbuf.at[2, u, at, :], dst_ref=wbuf.at[3, u, at, :],
            send_sem=fs.at[u, j], recv_sem=wr.at[3, u, j], device_id=core_dev, device_id_type=MESH,
        )

    def arrived(s, u, j):
        piece_copy(stem_out, s, u, j, ws.at[0], core_dev).wait_recv()

    def take_rest(u, pieces):
        for j in pieces:
            forward_core(u, j).start()

    tile[...] = (
        (div(iota((512, 128), 0), 128) == div(iota((512, 128), 1), 4))
        & (mod(iota((512, 128), 0), 4) == mod(iota((512, 128), 1), 4))
    ).astype(F32).astype(BF16)
    for copy in local_copies[3:5]:
        copy.wait()
    onehot = (iota((128, 64), 0) == ids[...]).astype(F32)
    emb[...] = dot(onehot.T.astype(BF16), table[...])
    local_copies[1].wait()
    local_copies[2].wait()
    patch_mask = div(iota((HALF, 128), 1), 4) == iota((HALF, 128), 0)

    def which(t):
        late = div(t, 4)
        second = div(t, 6)
        return (
            (1 - late) * div(t, 2) + late * (2 + mod(t, 2)),
            (1 - late) * mod(t, 2) + late * (odd_x + second - 2 * odd_x * second),
        )

    def constants():
        for l in range(LATENT):
            lane = iota((128, 1024), 1)
            want = div(mod(lane, WIDTH), HEAD) + l * HEADS + div(lane, WIDTH) * 64
            ex[l] = (iota((128, 1024), 0) == want).astype(F32).astype(BF16)
        for copy in local_copies[5:7]:
            copy.wait()
        qf = query[...].astype(F32)
        heads = iota((HEADS, WIDTH), 0) == div(iota((HEADS, WIDTH), 1), HEAD)
        qmat = jnp.concatenate(
            [jnp.where(heads, jnp.broadcast_to(qf[l:l + 1], (HEADS, WIDTH)), 0.0) for l in range(LATENT)],
            axis=0,
        ).astype(BF16)
        folded = dot_nt(qmat, kvw[:, :WIDTH]) * (LOG2E / HEAD**0.5)
        high = folded.astype(BF16).astype(F32)
        qk[...] = jnp.concatenate([high, folded - high], axis=0).T.astype(BF16)

    constants()

    def first_matrix(t):
        s, u = which(t)
        for k in range(3):
            @pl.when(t == (2, 4, 5)[k])
            def _():
                pixel_copy(k, 0, core_dev).wait_recv()
                stem_copy(k, core_dev).wait_recv()

        fscr[...] = pbuf[s, pl.ds(pl.multiple_of(u * CHUNK, CHUNK), CHUNK), :].astype(F32)
        for a in range(16):
            for i in range(4):
                row = jnp.broadcast_to(fscr[pl.ds(a * 4 + i, 1), :], (HALF, 128))
                lhs[pl.ds(a * HALF, HALF), pl.ds(i * 128, 128)] = jnp.where(
                    patch_mask, row, 0.0
                ).astype(BF16)
        pixels = dot(lhs[...], tile[...]).astype(BF16)[:, :16]
        h = dot(pixels, sbuf[s, u])
        stem = 0.5 * h * (1.0 + jnp.tanh(0.7978845608028654 * (h + 0.044715 * (h * h * h))))
        normed[t + div(t, 7)] = stem.astype(BF16)

    def second_matrix(t):
        s, u = which(t)

        @pl.when(t == 1)
        def _():
            for copy in held[:2]:
                copy.start()

        @pl.when(t == 2)
        def _():
            whole_copy(0, ws.at[0]).wait_recv()

        @pl.when(t == 3)
        def _():
            for j in range(2):
                arrived(2, odd_x, j)
                forward_x(j, (right, left)[j]).start()
            for copy in held[2:]:
                copy.start()
            take_rest(odd_x, range(2))
            whole_copy(1, ws.at[0]).wait_recv()

        @pl.when(t == 4)
        def _():
            for j in (2, 3):
                arrived(2, odd_x, j)
            take_rest(odd_x, (2, 3))

        @pl.when(t == 6)
        def _():
            for j in range(4):
                arrived(2, 1 - odd_x, j)
                forward_core(1 - odd_x, j).start()

        @pl.when((t == 5) | (t == 7))
        def _():
            for j in range(4):
                arrived(3, u, j)

    def project(t, src, at):
        s, u = which(t)
        tokens = dot(normed[src, at, :], wbuf[s, u]).astype(BF16).astype(F32)
        src_g = mod(s, 2)
        src_core = core + src_g - 2 * core * src_g
        up = div(s, 2)
        src_y = ylo + up - 2 * ylo * up
        var = (base + src_y * 2 + src_core) * 2 + u
        keyed = tokens + emb[pl.ds(var, 1), :]
        centre = jnp.mean(keyed, axis=-1, keepdims=True)
        away = keyed - centre
        spread = jnp.mean(away * away, axis=-1, keepdims=True)
        normed[t, at, :] = (away * lax.rsqrt(spread + 1e-05)).astype(BF16)

    def one_variable(t, carry):
        @pl.when(t < 8)
        def _():
            first_matrix(t)

        @pl.when(t > 0)
        def _():
            second_matrix(t - 1)

            @pl.when(t < 8)
            def _():
                project(t - 1, t - 1, pl.ds(0, 512))

        return carry

    lax.fori_loop(0, 9, one_variable, 0)
    last = jnp.int32(7)
    project(last, 8, pl.ds(pl.multiple_of(mod(z + 4, NZ) * CHUNK, CHUNK), CHUNK))

    low_lanes = iota((CHUNK, 128), 1) < 64

    def ring_copies(dr, d, half):
        off = mod(d + dr * (8 - 2 * d), 8)
        target = (mod(z + 1 + 6 * dr, NZ) * GROUP + g, bi)
        start = pl.multiple_of(half * HALF, HALF)
        return (
            pltpu.make_async_remote_copy(
                src_ref=ms.at[off, pl.ds(pl.multiple_of(half * 16, 16), 16), :], dst_ref=rms.at[dr, d - 1, half],
                send_sem=mss.at[dr, d - 1, half], recv_sem=msr.at[dr, d - 1, half],
                device_id=target, device_id_type=MESH,
            ),
            pltpu.make_async_remote_copy(
                src_ref=part.at[off, pl.ds(start, HALF), :], dst_ref=rpart.at[dr, d - 1, half],
                send_sem=os.at[dr, d - 1, half], recv_sem=orr.at[dr, d - 1, half],
                device_id=target, device_id_type=MESH,
            ),
        )

    def ring_send(dr, d, half):
        for copy in ring_copies(dr, d, half):
            copy.start()

    def put_level(off, half, level):
        ms[off, pl.ds(pl.multiple_of(half * 16, 16), 16), :] = jnp.where(low_lanes[:16], level[:16], level[16:])

    def both_lanes(packed):
        turned = pltpu.roll(packed, 64, 1)
        low = low_lanes[:16]
        return [jnp.where(low, packed, turned), jnp.where(low, turned, packed)]

    def local(off):
        start = pl.multiple_of(mod(z + off, NZ) * CHUNK, CHUNK)
        nb = normed[:8, pl.ds(start, CHUNK), :].reshape(8 * CHUNK, WIDTH)
        scores = dot(nb, qk[...])
        scores = (scores + pltpu.roll(scores, 64, 1)).reshape(8, CHUNK, 128)
        top = jnp.max(scores, axis=0)
        level = top + jnp.log2(jnp.sum(jnp.exp2(scores - top[None]), axis=0))
        p = jnp.exp2(scores - jnp.ceil(level)[None])
        put_level(off, 0, level[:HALF])
        put_level(off, 1, level[HALF:])
        pb = p.astype(BF16).reshape(8 * CHUNK, 128)
        values = dot(nb, kvw[:, WIDTH:])
        for l in range(LATENT):
            wide = dot(pb, ex[l, :, :WIDTH])
            part[off, :, l * WIDTH:(l + 1) * WIDTH] = jnp.sum(
                (wide * values).reshape(8, CHUNK, WIDTH), axis=0
            ).astype(BF16)

    def offset(dr, d):
        return mod(d + dr * (8 - 2 * d), 8)

    def incoming(d, i):
        for dr, h in ((0, 1 - i), (1, i)):
            for copy in ring_copies(dr, d + 1, h):
                copy.wait_recv()
        parts = []
        for dr, h in ((0, 1 - i), (1, i)):
            parts.append((dr, h, offset(dr, d), pl.ds(pl.multiple_of(h * HALF, HALF), HALF)))
        mine, other = [], []
        for dr, h, off, _ in parts:
            mine += both_lanes(ms[off, pl.ds(pl.multiple_of(h * 16, 16), 16), :])
            other += both_lanes(rms[dr, d, h])
        level1 = jnp.concatenate(mine, axis=0)
        level2 = jnp.concatenate(other, axis=0)
        m1 = jnp.ceil(level1)
        m2 = jnp.ceil(level2)
        top = jnp.maximum(m1, m2)
        level = top + jnp.log2(jnp.exp2(level1 - top) + jnp.exp2(level2 - top))
        m = jnp.ceil(level)
        return parts, level, jnp.exp2(m1 - m), jnp.exp2(m2 - m)

    def merge(d, i):
        parts, level, a1, a2 = incoming(d, i)
        ab = jnp.where(low_lanes, a2, a1).astype(BF16)
        for k, (_, h, off, _) in enumerate(parts):
            put_level(off, h, level[k * HALF:(k + 1) * HALF])
        for l in range(LATENT):
            cols = slice(l * WIDTH, (l + 1) * WIDTH)
            factor = dot(ab, ex[l])
            for k, (dr, h, off, at) in enumerate(parts):
                lines = slice(k * HALF, (k + 1) * HALF)
                part[off, at, cols] = (
                    factor[lines, :WIDTH] * rpart[dr, d, h, :, cols].astype(F32)
                    + factor[lines, WIDTH:] * part[off, at, cols].astype(F32)
                ).astype(BF16)

    def one_chunk(k, carry):
        odd = mod(k, 2)
        d = 3 - div(k - 2, 2)
        i = mod(k, 2)

        @pl.when(k < 8)
        def _():
            local(4 - div(k + 1, 2) * odd + div(k, 2) * (1 - odd))

        @pl.when(k == 0)
        def _():
            ring_send(0, 4, 0)
            ring_send(1, 4, 1)
            project(last, 8, pl.ds(0, 512))

        @pl.when(k > 2)
        def _():
            merge(d, i)

        @pl.when((k > 1) & (k < 8))
        def _():
            ring_send(0, d, 1 - i)
            ring_send(1, d, i)

        return carry

    lax.fori_loop(0, 9, one_chunk, 0)

    local_copies[7].wait()
    ones = jnp.ones((128, 128), F32)
    same_tile = div(iota((128, 128), 0), 16) == div(iota((128, 128), 1), 16)
    slot_row = iota((128, 128), 0)
    tile_lane = div(iota((128, 128), 1), 16)
    dest = iota((NVAR, 128), 0)
    dest_region = (div(dest, 4) * GROUP + g) * NBAND + mod(dest, 4) * 2 + yhi
    picked = jnp.zeros((NVAR, 128), F32)

    def slots(row):
        across = row.astype(F32) * ones
        below = jnp.where((across.T < across) & same_tile, 0.5, 0.0)
        return jnp.sum(below, axis=0, keepdims=True).astype(I32)

    for k in range(GROUP):
        row = regions[pl.ds(base + k, 1), :]
        hit = (slots(row) == mod(slot_row, 8)) & (div(slot_row, 32) == k) & (
            tile_lane == x * 2 + mod(div(slot_row, 16), 2)
        )
        in_region = (row == dest_region).astype(F32).astype(BF16)
        picked = picked + dot_nt(in_region, jnp.where(hit, 0.5, 0.0).astype(BF16))
    upper = mod(div(iota((NVAR, 128), 1), 8), 2) == 1
    chosen[...] = jnp.concatenate(
        [jnp.where(upper, 0.0, picked), jnp.where(upper, picked, 0.0)], axis=0
    ).astype(BF16)
    own_row = regions[pl.ds(vi, 1), :]
    own_hit = (slots(own_row) == iota((8, 128), 0)) & (div(iota((8, 128), 1), 16) == bi)
    cell = div(mod(iota((128, CHUNK), 1), HALF), 2)
    average = jnp.where(mod(iota((128, CHUNK), 0), 16) == cell, 0.25, 0.0).astype(BF16)
    pair_mean = dot(own_hit.astype(F32).astype(BF16), average).astype(BF16)
    region = vi * NBAND + bi
    count = jnp.sum((regions[...] == region).astype(F32))

    _, level, a1, a2 = incoming(0, 1)
    weight = jnp.where(low_lanes, a2, a1) * jnp.exp2(jnp.ceil(level) - level)
    weight_high = weight.astype(BF16).astype(F32)
    ab = jnp.concatenate([weight_high, weight - weight_high], axis=0).astype(BF16)
    mixed = []
    for l in range(LATENT):
        cols = slice(l * WIDTH, (l + 1) * WIDTH)
        factor = dot(ab, ex[l])
        factor = factor[:CHUNK] + factor[CHUNK:]
        received = jnp.concatenate([rpart[0, 0, 0, :, cols], rpart[1, 0, 1, :, cols]], axis=0)
        mixed.append(
            (factor[:, :WIDTH] * received.astype(F32)
             + factor[:, WIDTH:] * part[0, :, cols].astype(F32)).astype(BF16)
        )
    local_copies[8].wait()
    projected = dot(jnp.concatenate(mixed, axis=0), outw[...])
    sums = []
    for l in range(LATENT):
        cols = slice(l * WIDTH, (l + 1) * WIDTH)
        out = (projected[l * CHUNK:(l + 1) * CHUNK] + query[l:l + 1].astype(F32)).astype(BF16)
        lat[:, cols] = out
        sums.append(dot(pair_mean, out))
    pairs[member] = jnp.concatenate(
        [jnp.concatenate(sums[:2], axis=1), jnp.concatenate(sums[2:], axis=1)], axis=0
    ).astype(BF16)

    def pair_copy(j, slot):
        return pltpu.make_async_remote_copy(
            src_ref=pairs.at[slot], dst_ref=pairs.at[slot], send_sem=cs.at[j], recv_sem=cr.at[j],
            device_id=member_dev(j), device_id_type=MESH,
        )

    order = (1, 3, 5, 4, 7, 6, 2)
    for j in order:
        pair_copy(j, member).start()
    for j in order:
        other = (flip(ylo, j // 4) * 2 + flip(core, (j // 2) % 2)) * 2 + flip(yhi, j % 2)
        pair_copy(j, other).wait_recv()
    by_dest = dot(chosen[...], pairs[...].reshape(128, 2 * WIDTH))
    for k in range(16):
        table_f[:, k, :] = by_dest[(k // 8) * NVAR:(k // 8 + 1) * NVAR, (k % 8) * 128:(k % 8 + 1) * 128]
    table_b[...] = table_f[...].astype(BF16)

    def row_copy(i):
        to_z, to_x = place_off(i)
        return pltpu.make_async_remote_copy(
            src_ref=table_b.at[to_z * 4 + to_x], dst_ref=rows.at[i], send_sem=ts.at[i],
            recv_sem=tr.at[i], device_id=(to_z * GROUP + g, to_x * 2 + yhi), device_id_type=MESH,
        )

    def row_send(j, carry):
        row_copy(j).start()
        return carry

    def row_wait(j, carry):
        row_copy(j).wait_recv()
        return carry

    lax.fori_loop(0, NVAR - 1, row_send, 0)
    rows[NVAR - 1] = table_b[z * 4 + x]
    for copy in sends:
        copy.wait_send()
    for j in range(2):
        forward_x(j, (right, left)[j]).wait_send()
    for j in range(4):
        forward_core(0, j).wait_send()
        forward_core(1, j).wait_send()

    def ring_over(i, carry):
        dr = mod(i, 2)
        half = mod(div(i, 2), 2)
        d = 1 + div(i, 4)

        @pl.when((d < 4) | (half == dr))
        def _():
            for copy in ring_copies(dr, d, half):
                copy.wait_send()

        return carry

    for j in order:
        pair_copy(j, member).wait_send()

    def row_over(j, carry):
        row_copy(j).wait_send()
        return carry

    lax.fori_loop(0, 16, ring_over, 0)
    lax.fori_loop(0, NVAR - 1, row_over, 0)
    lax.fori_loop(0, NVAR - 1, row_wait, 0)
    total = jnp.sum(rows[...].astype(F32), axis=0) / count
    for l in range(LATENT):
        for k in range(4):
            means[0, l:l + 1, k * 128:(k + 1) * 128] = total[l * 4 + k:l * 4 + k + 1, :]


def shards(fields, stem_in, stem_out, level_ids, level_table, latent_query, kv_weight, out_weight, region_ids):
    vmem = pl.BlockSpec(memory_space=pltpu.VMEM)
    dma = pltpu.SemaphoreType.DMA
    lat, means = pl.pallas_call(
        kernel,
        out_shape=(
            jax.ShapeDtypeStruct((CHUNK, FLAT), BF16),
            jax.ShapeDtypeStruct((1, LATENT, WIDTH), F32),
        ),
        in_specs=[pl.BlockSpec(memory_space=pl.ANY)] * 9,
        out_specs=(vmem, vmem),
        scratch_shapes=[
            pltpu.VMEM((2, 256, 128), BF16),
            pltpu.VMEM((1, 64), I32),
            pltpu.VMEM((128, WIDTH), BF16),
            pltpu.VMEM((LATENT, WIDTH), BF16),
            pltpu.VMEM((WIDTH, 2 * WIDTH), BF16),
            pltpu.VMEM((WIDTH, WIDTH), BF16),
            pltpu.VMEM((32, 128), I32),
            pltpu.VMEM((GROUP, 128, 128), BF16),
            pltpu.VMEM((GROUP, 128, 128), BF16),
            pltpu.VMEM((GROUP, 2, 16, WIDTH), BF16),
            pltpu.VMEM((GROUP, 2, WIDTH, WIDTH), BF16),
            pltpu.VMEM((CHUNK, 128), F32),
            pltpu.VMEM((512, 512), BF16),
            pltpu.VMEM((512, 128), BF16),
            pltpu.VMEM((9, 512, WIDTH), BF16),
            pltpu.VMEM((64, WIDTH), F32),
            pltpu.VMEM((WIDTH, 128), BF16),
            pltpu.VMEM((LATENT, 128, 2 * WIDTH), BF16),
            pltpu.VMEM((NZ, CHUNK, FLAT), BF16),
            pltpu.VMEM((NZ, HALF, 128), F32),
            pltpu.VMEM((2, 4, 2, HALF, FLAT), BF16),
            pltpu.VMEM((2, 4, 2, 16, 128), F32),
            pltpu.VMEM((2 * NVAR, 128), BF16),
            pltpu.VMEM((8, 16, 2 * WIDTH), BF16),
            pltpu.VMEM((NVAR, 16, 128), F32),
            pltpu.VMEM((NVAR, 16, 128), BF16),
            pltpu.VMEM((NVAR, 16, 128), BF16),
            dma((9,)),
            dma((3,)), dma((3,)),
            dma((3,)), dma((3,)),
            dma((8,)), dma((GROUP, 2, 4)), dma((2,)), dma((2, 4)),
            dma((2, 4, 2)), dma((2, 4, 2)),
            dma((2, 4, 2)), dma((2, 4, 2)),
            dma((8,)), dma((8,)),
            dma((NVAR,)), dma((NVAR,)),
        ],
        compiler_params=pltpu.CompilerParams(
            collective_id=0, has_side_effects=True, vmem_limit_bytes=60 * 1024 * 1024
        ),
        name="window",
    )(
        fields, stem_in, stem_out, level_ids.reshape(1, -1), level_table, latent_query,
        kv_weight, out_weight, region_ids,
    )
    return lat.reshape(2, 32, LATENT, WIDTH), means


def solution(mesh):
    in_specs = (
        P("var", None, "band"),
        P("var", None, None),
        P("var", None, None),
        P(),
        P(),
        P(),
        P(),
        P(),
        P(),
    )
    out_specs = (P("var", "band", None, None), P(("var", "band"), None, None))
    return jax.shard_map(shards, mesh=mesh, in_specs=in_specs, out_specs=out_specs, check_vma=False)
```

```python
import jax
import jax.numpy as jnp
from jax import lax
from jax.experimental import pallas as pl
from jax.experimental.pallas import tpu as pltpu
from jax.sharding import PartitionSpec as P

MESH = pl.DeviceIdType.MESH
BF16 = jnp.bfloat16
F32 = jnp.float32
I32 = jnp.int32

HEADS = 16
HEAD = 32
WIDTH = 512
LATENT = 4
FLAT = LATENT * WIDTH
NZ = 8
GROUP = 4
NVAR = 32
NBAND = 8
CHUNK = 64
HALF = 32
LOG2E = 1.4426950408889634
PIECES = ((0, 128), (128, 128), (256, 128), (384, 128))


def iota(shape, axis):
    return lax.broadcasted_iota(I32, shape, axis)


def dot(a, b):
    return jnp.dot(a, b, preferred_element_type=F32)


def dot_nt(a, b):
    return lax.dot_general(a, b, (((1,), (1,)), ((), ())), preferred_element_type=F32)


def mod(a, n):
    return lax.rem(a, jnp.int32(n))


def div(a, n):
    return lax.div(a, jnp.int32(n))


def kernel(
    fields, stem_in, stem_out, ids_hbm, table_hbm, query_hbm, kvw_hbm, outw_hbm, regions_hbm,
    lat, means,
    field_v, ids, table, query, kvw, outw, regions,
    pbuf, pown, sbuf, wbuf, fscr, lhs, tile, normed, emb, qk, ex,
    part, ms, rpart, rms, chosen, pairs, table_f, table_b, rows,
    lsem, ps, pr, ss, sr, ws, wr, xs, fs, os, orr, mss, msr, cs, cr, ts, tr,
):
    vi = lax.axis_index("var")
    bi = lax.axis_index("band")
    z = div(vi, GROUP)
    g = mod(vi, GROUP)
    ylo = div(g, 2)
    core = mod(g, 2)
    x = div(bi, 2)
    yhi = mod(bi, 2)
    y = yhi * 2 + ylo
    odd_x = mod(x, 2)
    base = z * GROUP
    g_core = ylo * 2 + 1 - core
    g_y = (1 - ylo) * 2 + core
    g_diag = (1 - ylo) * 2 + 1 - core
    core_dev = (base + g_core, bi)
    band_next = x * 2 + div(mod(y + 1, 4), 2)
    band_prev = x * 2 + div(mod(y + 3, 4), 2)
    band_far = x * 2 + 1 - yhi
    right = (vi, mod(x + 1, 4) * 2 + yhi)
    left = (vi, mod(x + 3, 4) * 2 + yhi)
    member = g * 2 + yhi

    def flip(bit, by):
        return mod(bit + by, 2)

    def member_dev(j):
        other = flip(ylo, j // 4) * 2 + flip(core, (j // 2) % 2)
        return (base + other, x * 2 + flip(yhi, j % 2))

    def place_off(i):
        a, b = div(i, 4), mod(i, 4)
        da = 4 - div(a + 1, 2) * mod(a, 2) + div(a, 2) * (1 - mod(a, 2))
        db = 2 - div(b + 1, 2) * mod(b, 2) + div(b, 2) * (1 - mod(b, 2))
        return mod(z + da, NZ), mod(x + db, 4)

    barrier = pltpu.get_barrier_semaphore()
    near = [member_dev(j) for j in (2, 4, 5, 6, 7)]
    near += [right, left]
    near += [(mod(z + j, NZ) * GROUP + g, bi) for j in (1, NZ - 1)]
    for device in near:
        pl.semaphore_signal(barrier, inc=1, device_id=device, device_id_type=MESH)

    local_copies = [
        pltpu.make_async_copy(src, dst, lsem.at[k])
        for k, (src, dst) in enumerate((
            (fields, field_v), (stem_out, wbuf.at[0]), (stem_in, sbuf.at[0]), (ids_hbm, ids),
            (table_hbm, table), (query_hbm, query), (kvw_hbm, kvw), (regions_hbm, regions),
            (outw_hbm, outw),
        ))
    ]
    for copy in local_copies:
        copy.start()

    pl.semaphore_wait(barrier, len(near))

    def piece_copy(src, s, u, j, send, target):
        at = pl.ds(*PIECES[j])
        return pltpu.make_async_remote_copy(
            src_ref=src.at[u, at, :], dst_ref=wbuf.at[s, u, at, :],
            send_sem=send, recv_sem=wr.at[s, u, j], device_id=target, device_id_type=MESH,
        )

    def whole_copy(u, send):
        return pltpu.make_async_remote_copy(
            src_ref=stem_out.at[u], dst_ref=wbuf.at[1, u], send_sem=send,
            recv_sem=wr.at[1, u, 0], device_id=core_dev, device_id_type=MESH,
        )

    def pixel_copy(k, source, target):
        return pltpu.make_async_remote_copy(
            src_ref=pown.at[source], dst_ref=pbuf.at[k + 1], send_sem=ps.at[k],
            recv_sem=pr.at[k], device_id=target, device_id_type=MESH,
        )

    def stem_copy(k, target):
        return pltpu.make_async_remote_copy(
            src_ref=stem_in, dst_ref=sbuf.at[k + 1], send_sem=ss.at[k],
            recv_sem=sr.at[k], device_id=target, device_id_type=MESH,
        )

    next_dev = (base + g_y, band_next)
    prev_dev = (base + g_y, band_prev)
    sends = [
        piece_copy(stem_out, 2, odd_x, 0, ws.at[0], next_dev),
        piece_copy(stem_out, 2, odd_x, 1, ws.at[1], prev_dev),
        whole_copy(0, ws.at[6]),
        stem_copy(0, core_dev),
        stem_copy(1, (base + g_y, band_far)),
        stem_copy(2, (base + g_diag, band_far)),
        whole_copy(1, ws.at[7]),
    ]
    later = [
        pixel_copy(0, g_core, core_dev),
        pixel_copy(1, g_y, (base + g_y, bi)),
        pixel_copy(2, g_diag, (base + g_diag, bi)),
    ]
    for copy in sends:
        copy.start()
    local_copies[0].wait()
    ff = field_v[...].astype(F32).reshape(2, NZ, GROUP, 8, 128)
    for k in range(GROUP):
        pown[k] = ff[:, :, k].reshape(2 * NZ * 8, 128).astype(BF16)
    for copy in later:
        copy.start()
    held = [
        piece_copy(stem_out, 2, odd_x, 2, ws.at[2], next_dev),
        piece_copy(stem_out, 2, odd_x, 3, ws.at[3], prev_dev),
        piece_copy(stem_out, 2, 1 - odd_x, 2, ws.at[4], next_dev),
        piece_copy(stem_out, 2, 1 - odd_x, 3, ws.at[5], prev_dev),
    ]
    sends = sends + later + held
    pbuf[0] = pown[g]

    def forward_x(j, target):
        return piece_copy(wbuf.at[2], 2, odd_x, j, xs.at[j], target)

    def forward_core(u, j):
        at = pl.ds(*PIECES[j])
        return pltpu.make_async_remote_copy(
            src_ref=wbuf.at[2, u, at, :], dst_ref=wbuf.at[3, u, at, :],
            send_sem=fs.at[u, j], recv_sem=wr.at[3, u, j], device_id=core_dev, device_id_type=MESH,
        )

    def arrived(s, u, j):
        piece_copy(stem_out, s, u, j, ws.at[0], core_dev).wait_recv()

    def take_rest(u, pieces):
        for j in pieces:
            forward_core(u, j).start()

    tile[...] = (
        (div(iota((512, 128), 0), 128) == div(iota((512, 128), 1), 4))
        & (mod(iota((512, 128), 0), 4) == mod(iota((512, 128), 1), 4))
    ).astype(F32).astype(BF16)
    for copy in local_copies[3:5]:
        copy.wait()
    onehot = (iota((128, 64), 0) == ids[...]).astype(F32)
    emb[...] = dot(onehot.T.astype(BF16), table[...])
    local_copies[1].wait()
    local_copies[2].wait()
    patch_mask = div(iota((HALF, 128), 1), 4) == iota((HALF, 128), 0)

    def which(t):
        late = div(t, 4)
        second = div(t, 6)
        return (
            (1 - late) * div(t, 2) + late * (2 + mod(t, 2)),
            (1 - late) * mod(t, 2) + late * (odd_x + second - 2 * odd_x * second),
        )

    def constants():
        for l in range(LATENT):
            lane = iota((128, 1024), 1)
            want = div(mod(lane, WIDTH), HEAD) + l * HEADS + div(lane, WIDTH) * 64
            ex[l] = (iota((128, 1024), 0) == want).astype(F32).astype(BF16)
        for copy in local_copies[5:7]:
            copy.wait()
        qf = query[...].astype(F32)
        heads = iota((HEADS, WIDTH), 0) == div(iota((HEADS, WIDTH), 1), HEAD)
        qmat = jnp.concatenate(
            [jnp.where(heads, jnp.broadcast_to(qf[l:l + 1], (HEADS, WIDTH)), 0.0) for l in range(LATENT)],
            axis=0,
        ).astype(BF16)
        folded = dot_nt(qmat, kvw[:, :WIDTH]) * (LOG2E / HEAD**0.5)
        high = folded.astype(BF16).astype(F32)
        qk[...] = jnp.concatenate([high, folded - high], axis=0).T.astype(BF16)

    constants()

    def first_matrix(t):
        s, u = which(t)
        for k in range(3):
            @pl.when(t == (2, 4, 5)[k])
            def _():
                pixel_copy(k, 0, core_dev).wait_recv()
                stem_copy(k, core_dev).wait_recv()

        fscr[...] = pbuf[s, pl.ds(pl.multiple_of(u * CHUNK, CHUNK), CHUNK), :].astype(F32)
        for a in range(16):
            for i in range(4):
                row = jnp.broadcast_to(fscr[pl.ds(a * 4 + i, 1), :], (HALF, 128))
                lhs[pl.ds(a * HALF, HALF), pl.ds(i * 128, 128)] = jnp.where(
                    patch_mask, row, 0.0
                ).astype(BF16)
        pixels = dot(lhs[...], tile[...]).astype(BF16)[:, :16]
        h = dot(pixels, sbuf[s, u])
        stem = 0.5 * h * (1.0 + jnp.tanh(0.7978845608028654 * (h + 0.044715 * (h * h * h))))
        normed[t + div(t, 7)] = stem.astype(BF16)

    def second_matrix(t):
        s, u = which(t)

        @pl.when(t == 1)
        def _():
            for copy in held[:2]:
                copy.start()

        @pl.when(t == 2)
        def _():
            whole_copy(0, ws.at[0]).wait_recv()

        @pl.when(t == 3)
        def _():
            for j in range(2):
                arrived(2, odd_x, j)
                forward_x(j, (right, left)[j]).start()
            for copy in held[2:]:
                copy.start()
            take_rest(odd_x, range(2))
            whole_copy(1, ws.at[0]).wait_recv()

        @pl.when(t == 4)
        def _():
            for j in (2, 3):
                arrived(2, odd_x, j)
            take_rest(odd_x, (2, 3))

        @pl.when(t == 6)
        def _():
            for j in range(4):
                arrived(2, 1 - odd_x, j)
                forward_core(1 - odd_x, j).start()

        @pl.when((t == 5) | (t == 7))
        def _():
            for j in range(4):
                arrived(3, u, j)

    def project(t, src, at):
        s, u = which(t)
        tokens = dot(normed[src, at, :], wbuf[s, u]).astype(BF16).astype(F32)
        src_g = mod(s, 2)
        src_core = core + src_g - 2 * core * src_g
        up = div(s, 2)
        src_y = ylo + up - 2 * ylo * up
        var = (base + src_y * 2 + src_core) * 2 + u
        keyed = tokens + emb[pl.ds(var, 1), :]
        centre = jnp.mean(keyed, axis=-1, keepdims=True)
        away = keyed - centre
        spread = jnp.mean(away * away, axis=-1, keepdims=True)
        normed[t, at, :] = (away * lax.rsqrt(spread + 1e-05)).astype(BF16)

    def one_variable(t, carry):
        @pl.when(t < 8)
        def _():
            first_matrix(t)

        @pl.when(t > 0)
        def _():
            second_matrix(t - 1)

            @pl.when(t < 8)
            def _():
                project(t - 1, t - 1, pl.ds(0, 512))

        return carry

    lax.fori_loop(0, 9, one_variable, 0)
    last = jnp.int32(7)
    project(last, 8, pl.ds(pl.multiple_of(mod(z + 4, NZ) * CHUNK, CHUNK), CHUNK))

    low_lanes = iota((CHUNK, 128), 1) < 64

    def ring_copies(dr, d, half):
        off = mod(d + dr * (8 - 2 * d), 8)
        target = (mod(z + 1 + 6 * dr, NZ) * GROUP + g, bi)
        start = pl.multiple_of(half * HALF, HALF)
        return (
            pltpu.make_async_remote_copy(
                src_ref=ms.at[off, pl.ds(pl.multiple_of(half * 16, 16), 16), :], dst_ref=rms.at[dr, d - 1, half],
                send_sem=mss.at[dr, d - 1, half], recv_sem=msr.at[dr, d - 1, half],
                device_id=target, device_id_type=MESH,
            ),
            pltpu.make_async_remote_copy(
                src_ref=part.at[off, pl.ds(start, HALF), :], dst_ref=rpart.at[dr, d - 1, half],
                send_sem=os.at[dr, d - 1, half], recv_sem=orr.at[dr, d - 1, half],
                device_id=target, device_id_type=MESH,
            ),
        )

    def ring_send(dr, d, half):
        for copy in ring_copies(dr, d, half):
            copy.start()

    def put_level(off, half, level):
        ms[off, pl.ds(pl.multiple_of(half * 16, 16), 16), :] = jnp.where(low_lanes[:16], level[:16], level[16:])

    def both_lanes(packed):
        turned = pltpu.roll(packed, 64, 1)
        low = low_lanes[:16]
        return [jnp.where(low, packed, turned), jnp.where(low, turned, packed)]

    def local(off):
        start = pl.multiple_of(mod(z + off, NZ) * CHUNK, CHUNK)
        nb = normed[:8, pl.ds(start, CHUNK), :].reshape(8 * CHUNK, WIDTH)
        scores = dot(nb, qk[...])
        scores = (scores + pltpu.roll(scores, 64, 1)).reshape(8, CHUNK, 128)
        top = jnp.max(scores, axis=0)
        level = top + jnp.log2(jnp.sum(jnp.exp2(scores - top[None]), axis=0))
        p = jnp.exp2(scores - jnp.ceil(level)[None])
        put_level(off, 0, level[:HALF])
        put_level(off, 1, level[HALF:])
        pb = p.astype(BF16).reshape(8 * CHUNK, 128)
        values = dot(nb, kvw[:, WIDTH:])
        for l in range(LATENT):
            wide = dot(pb, ex[l, :, :WIDTH])
            part[off, :, l * WIDTH:(l + 1) * WIDTH] = jnp.sum(
                (wide * values).reshape(8, CHUNK, WIDTH), axis=0
            ).astype(BF16)

    def offset(dr, d):
        return mod(d + dr * (8 - 2 * d), 8)

    def incoming(d, i):
        for dr, h in ((0, 1 - i), (1, i)):
            for copy in ring_copies(dr, d + 1, h):
                copy.wait_recv()
        parts = []
        for dr, h in ((0, 1 - i), (1, i)):
            parts.append((dr, h, offset(dr, d), pl.ds(pl.multiple_of(h * HALF, HALF), HALF)))
        mine, other = [], []
        for dr, h, off, _ in parts:
            mine += both_lanes(ms[off, pl.ds(pl.multiple_of(h * 16, 16), 16), :])
            other += both_lanes(rms[dr, d, h])
        level1 = jnp.concatenate(mine, axis=0)
        level2 = jnp.concatenate(other, axis=0)
        m1 = jnp.ceil(level1)
        m2 = jnp.ceil(level2)
        top = jnp.maximum(m1, m2)
        level = top + jnp.log2(jnp.exp2(level1 - top) + jnp.exp2(level2 - top))
        m = jnp.ceil(level)
        return parts, level, jnp.exp2(m1 - m), jnp.exp2(m2 - m)

    def merge(d, i):
        parts, level, a1, a2 = incoming(d, i)
        ab = jnp.where(low_lanes, a2, a1).astype(BF16)
        for k, (_, h, off, _) in enumerate(parts):
            put_level(off, h, level[k * HALF:(k + 1) * HALF])
        for l in range(LATENT):
            cols = slice(l * WIDTH, (l + 1) * WIDTH)
            factor = dot(ab, ex[l])
            for k, (dr, h, off, at) in enumerate(parts):
                lines = slice(k * HALF, (k + 1) * HALF)
                part[off, at, cols] = (
                    factor[lines, :WIDTH] * rpart[dr, d, h, :, cols].astype(F32)
                    + factor[lines, WIDTH:] * part[off, at, cols].astype(F32)
                ).astype(BF16)

    def one_chunk(k, carry):
        odd = mod(k, 2)
        d = 3 - div(k - 2, 2)
        i = mod(k, 2)

        @pl.when(k < 8)
        def _():
            local(4 - div(k + 1, 2) * odd + div(k, 2) * (1 - odd))

        @pl.when(k == 0)
        def _():
            ring_send(0, 4, 0)
            ring_send(1, 4, 1)
            project(last, 8, pl.ds(0, 512))

        @pl.when(k > 2)
        def _():
            merge(d, i)

        @pl.when((k > 1) & (k < 8))
        def _():
            ring_send(0, d, 1 - i)
            ring_send(1, d, i)

        return carry

    lax.fori_loop(0, 9, one_chunk, 0)

    local_copies[7].wait()
    ones = jnp.ones((128, 128), F32)
    same_tile = div(iota((128, 128), 0), 16) == div(iota((128, 128), 1), 16)
    slot_row = iota((128, 128), 0)
    tile_lane = div(iota((128, 128), 1), 16)
    dest = iota((NVAR, 128), 0)
    dest_region = (div(dest, 4) * GROUP + g) * NBAND + mod(dest, 4) * 2 + yhi
    picked = jnp.zeros((NVAR, 128), F32)

    def slots(row):
        across = row.astype(F32) * ones
        below = jnp.where((across.T < across) & same_tile, 0.5, 0.0)
        return jnp.sum(below, axis=0, keepdims=True).astype(I32)

    for k in range(GROUP):
        row = regions[pl.ds(base + k, 1), :]
        hit = (slots(row) == mod(slot_row, 8)) & (div(slot_row, 32) == k) & (
            tile_lane == x * 2 + mod(div(slot_row, 16), 2)
        )
        in_region = (row == dest_region).astype(F32).astype(BF16)
        picked = picked + dot_nt(in_region, jnp.where(hit, 0.5, 0.0).astype(BF16))
    upper = mod(div(iota((NVAR, 128), 1), 8), 2) == 1
    chosen[...] = jnp.concatenate(
        [jnp.where(upper, 0.0, picked), jnp.where(upper, picked, 0.0)], axis=0
    ).astype(BF16)
    own_row = regions[pl.ds(vi, 1), :]
    own_hit = (slots(own_row) == iota((8, 128), 0)) & (div(iota((8, 128), 1), 16) == bi)
    cell = div(mod(iota((128, CHUNK), 1), HALF), 2)
    average = jnp.where(mod(iota((128, CHUNK), 0), 16) == cell, 0.25, 0.0).astype(BF16)
    pair_mean = dot(own_hit.astype(F32).astype(BF16), average).astype(BF16)
    region = vi * NBAND + bi
    count = jnp.sum((regions[...] == region).astype(F32))

    _, level, a1, a2 = incoming(0, 1)
    weight = jnp.where(low_lanes, a2, a1) * jnp.exp2(jnp.ceil(level) - level)
    weight_high = weight.astype(BF16).astype(F32)
    ab = jnp.concatenate([weight_high, weight - weight_high], axis=0).astype(BF16)
    mixed = []
    for l in range(LATENT):
        cols = slice(l * WIDTH, (l + 1) * WIDTH)
        factor = dot(ab, ex[l])
        factor = factor[:CHUNK] + factor[CHUNK:]
        received = jnp.concatenate([rpart[0, 0, 0, :, cols], rpart[1, 0, 1, :, cols]], axis=0)
        mixed.append(
            (factor[:, :WIDTH] * received.astype(F32)
             + factor[:, WIDTH:] * part[0, :, cols].astype(F32)).astype(BF16)
        )
    local_copies[8].wait()
    projected = dot(jnp.concatenate(mixed, axis=0), outw[...])
    sums = []
    for l in range(LATENT):
        cols = slice(l * WIDTH, (l + 1) * WIDTH)
        out = (projected[l * CHUNK:(l + 1) * CHUNK] + query[l:l + 1].astype(F32)).astype(BF16)
        lat[:, cols] = out
        sums.append(dot(pair_mean, out))
    pairs[member] = jnp.concatenate(
        [jnp.concatenate(sums[:2], axis=1), jnp.concatenate(sums[2:], axis=1)], axis=0
    ).astype(BF16)

    def pair_copy(j, slot):
        return pltpu.make_async_remote_copy(
            src_ref=pairs.at[slot], dst_ref=pairs.at[slot], send_sem=cs.at[j], recv_sem=cr.at[j],
            device_id=member_dev(j), device_id_type=MESH,
        )

    order = (1, 3, 5, 4, 7, 6, 2)
    for j in order:
        pair_copy(j, member).start()
    for j in order:
        other = (flip(ylo, j // 4) * 2 + flip(core, (j // 2) % 2)) * 2 + flip(yhi, j % 2)
        pair_copy(j, other).wait_recv()
    by_dest = dot(chosen[...], pairs[...].reshape(128, 2 * WIDTH))
    for k in range(16):
        table_f[:, k, :] = by_dest[(k // 8) * NVAR:(k // 8 + 1) * NVAR, (k % 8) * 128:(k % 8 + 1) * 128]
    table_b[...] = table_f[...].astype(BF16)

    def row_copy(i):
        to_z, to_x = place_off(i)
        return pltpu.make_async_remote_copy(
            src_ref=table_b.at[to_z * 4 + to_x], dst_ref=rows.at[i], send_sem=ts.at[i],
            recv_sem=tr.at[i], device_id=(to_z * GROUP + g, to_x * 2 + yhi), device_id_type=MESH,
        )

    def row_send(j, carry):
        row_copy(j).start()
        return carry

    def row_wait(j, carry):
        row_copy(j).wait_recv()
        return carry

    lax.fori_loop(0, NVAR - 1, row_send, 0)
    rows[NVAR - 1] = table_b[z * 4 + x]
    for copy in sends:
        copy.wait_send()
    for j in range(2):
        forward_x(j, (right, left)[j]).wait_send()
    for j in range(4):
        forward_core(0, j).wait_send()
        forward_core(1, j).wait_send()

    def ring_over(i, carry):
        dr = mod(i, 2)
        half = mod(div(i, 2), 2)
        d = 1 + div(i, 4)

        @pl.when((d < 4) | (half == dr))
        def _():
            for copy in ring_copies(dr, d, half):
                copy.wait_send()

        return carry

    for j in order:
        pair_copy(j, member).wait_send()

    def row_over(j, carry):
        row_copy(j).wait_send()
        return carry

    lax.fori_loop(0, 16, ring_over, 0)
    lax.fori_loop(0, NVAR - 1, row_over, 0)
    lax.fori_loop(0, NVAR - 1, row_wait, 0)
    total = jnp.sum(rows[...].astype(F32), axis=0) / count
    for l in range(LATENT):
        for k in range(4):
            means[0, l:l + 1, k * 128:(k + 1) * 128] = total[l * 4 + k:l * 4 + k + 1, :]


def shards(fields, stem_in, stem_out, level_ids, level_table, latent_query, kv_weight, out_weight, region_ids):
    vmem = pl.BlockSpec(memory_space=pltpu.VMEM)
    dma = pltpu.SemaphoreType.DMA
    lat, means = pl.pallas_call(
        kernel,
        out_shape=(
            jax.ShapeDtypeStruct((CHUNK, FLAT), BF16),
            jax.ShapeDtypeStruct((1, LATENT, WIDTH), F32),
        ),
        in_specs=[pl.BlockSpec(memory_space=pl.ANY)] * 9,
        out_specs=(vmem, vmem),
        scratch_shapes=[
            pltpu.VMEM((2, 256, 128), BF16),
            pltpu.VMEM((1, 64), I32),
            pltpu.VMEM((128, WIDTH), BF16),
            pltpu.VMEM((LATENT, WIDTH), BF16),
            pltpu.VMEM((WIDTH, 2 * WIDTH), BF16),
            pltpu.VMEM((WIDTH, WIDTH), BF16),
            pltpu.VMEM((32, 128), I32),
            pltpu.VMEM((GROUP, 128, 128), BF16),
            pltpu.VMEM((GROUP, 128, 128), BF16),
            pltpu.VMEM((GROUP, 2, 16, WIDTH), BF16),
            pltpu.VMEM((GROUP, 2, WIDTH, WIDTH), BF16),
            pltpu.VMEM((CHUNK, 128), F32),
            pltpu.VMEM((512, 512), BF16),
            pltpu.VMEM((512, 128), BF16),
            pltpu.VMEM((9, 512, WIDTH), BF16),
            pltpu.VMEM((64, WIDTH), F32),
            pltpu.VMEM((WIDTH, 128), BF16),
            pltpu.VMEM((LATENT, 128, 2 * WIDTH), BF16),
            pltpu.VMEM((NZ, CHUNK, FLAT), BF16),
            pltpu.VMEM((NZ, HALF, 128), F32),
            pltpu.VMEM((2, 4, 2, HALF, FLAT), BF16),
            pltpu.VMEM((2, 4, 2, 16, 128), F32),
            pltpu.VMEM((2 * NVAR, 128), BF16),
            pltpu.VMEM((8, 16, 2 * WIDTH), BF16),
            pltpu.VMEM((NVAR, 16, 128), F32),
            pltpu.VMEM((NVAR, 16, 128), BF16),
            pltpu.VMEM((NVAR, 16, 128), BF16),
            dma((9,)),
            dma((3,)), dma((3,)),
            dma((3,)), dma((3,)),
            dma((8,)), dma((GROUP, 2, 4)), dma((2,)), dma((2, 4)),
            dma((2, 4, 2)), dma((2, 4, 2)),
            dma((2, 4, 2)), dma((2, 4, 2)),
            dma((8,)), dma((8,)),
            dma((NVAR,)), dma((NVAR,)),
        ],
        compiler_params=pltpu.CompilerParams(
            collective_id=0, has_side_effects=True, vmem_limit_bytes=60 * 1024 * 1024
        ),
        name="window",
    )(
        fields, stem_in, stem_out, level_ids.reshape(1, -1), level_table, latent_query,
        kv_weight, out_weight, region_ids,
    )
    return lat.reshape(2, 32, LATENT, WIDTH), means


def solution(mesh):
    in_specs = (
        P("var", None, "band"),
        P("var", None, None),
        P("var", None, None),
        P(),
        P(),
        P(),
        P(),
        P(),
        P(),
    )
    out_specs = (P("var", "band", None, None), P(("var", "band"), None, None))
    return jax.shard_map(shards, mesh=mesh, in_specs=in_specs, out_specs=out_specs, check_vma=False)
```
